32 devices in a mesh: grp: 4 (over x, core), inner: 8 (over z, y).
Axes of the slice: x: 2, y: 2, z: 4, core: 2. Of those that a mesh axis runs over, the one named last changes fastest.
Arguments:
- moe_input: bfloat16 [4096, 2048], P(('grp', 'inner')), may hold values from -6 to 6
- out_grad: bfloat16 [4096, 2048], P(('grp', 'inner')), may hold values from -1.5 to 1.5
- context: bfloat16 [4096, 4096], P('grp', 'inner'), may hold values from -0.119628906 to 0.119628906
- gate_scale: float32 [32, 256], P(('grp', 'inner')), may hold values from 0.2 to 1
- selected: int32 [32, 256], replicated, may hold values from 0 to 4095, as said below
- w_gate: bfloat16 [32, 2048, 768], P(('grp', 'inner')), may hold values from -0.125 to 0.125
- w_up: bfloat16 [32, 2048, 768], P(('grp', 'inner')), may hold values from -0.125 to 0.125
- w_down: bfloat16 [32, 768, 2048], P(('grp', 'inner')), may hold values from -0.21875 to 0.21875
- w_out: bfloat16 [4096, 2048], P('inner'), may hold values from -0.09375 to 0.09375
Outputs:
- grad_gate: bfloat16 [32, 2048, 768], P(('grp', 'inner'))
- grad_up: bfloat16 [32, 2048, 768], P(('grp', 'inner'))
- grad_down: bfloat16 [32, 768, 2048], P(('grp', 'inner'))
- grad_context: bfloat16 [4096, 4096], P('grp', 'inner')
- grad_out: bfloat16 [4096, 2048], P('inner', 'grp')
The draws below stay inside these ranges and needn't reach their ends.
Inputs may be any that keep to these rules, and one draw needn't show every extreme that they name: `selected`: each expert's 256 token indices are distinct; at most 16 of them lie among the 128 tokens of one device (tokens d * 128 to (d + 1) * 128 - 1), and every expert takes exactly 16 from some device.
All inputs are finite; a program needn't handle non-finite values.
Results may differ from the reference program's by a relative error of at most 0.014.
Values may be sent and summed in bfloat16 or wider, within the bound.
A program may use at most 128 MiB of HBM per device.

```python
import math
import jax
import jax.numpy as jnp
from jax import lax

D = 2048
FF = 768
TOK_DEV = 128
CAP = 256
EXPERTS = 32
TOKENS = 4096
QDIM = 4096
MOST = 16


def draw_selected(key, part):
    devices = TOKENS // TOK_DEV
    items = devices * MOST
    first, second, third, fourth = jax.random.split(key, 4)
    item_ids = jnp.arange(items, dtype=jnp.int32)
    source_of = item_ids // MOST
    scores = jax.random.randint(first, (EXPERTS, items), 0, 1048576, dtype=jnp.int32) * items + item_ids[None, :]
    forced = jax.random.randint(second, (EXPERTS, 1), 0, devices, dtype=jnp.int32)
    favour = jax.random.randint(fourth, (devices,), 0, 4, dtype=jnp.int32) * 134217728
    scores = scores + jnp.where(source_of[None, :] == forced, 1073741824, 0) + favour[source_of][None, :]
    unused, chosen = lax.top_k(scores, CAP)
    source = chosen // MOST
    within = chosen % MOST
    base = jax.random.randint(third, (EXPERTS, devices), 0, TOK_DEV, dtype=jnp.int32)
    stride = TOK_DEV // MOST
    start = jnp.take_along_axis(base, source, axis=1)
    offset = (start + within * stride) % TOK_DEV
    return (source * TOK_DEV + offset).astype(jnp.int32)


def shard_levels(own_key, dims, pieces, least, largest):
    gain, own = 1.0, jax.random.fold_in(own_key, 6)
    for dim, blocks in pieces:
        heights = jnp.exp(jax.random.uniform(jax.random.fold_in(own, dim), (blocks,), jnp.float32, least / len(pieces), largest / len(pieces)))
        gain = gain * jnp.repeat(heights, dims[dim] // blocks).reshape([-1 if axis == dim else 1 for axis in range(len(dims))])
    return gain


def bell_draw(key, extent, scale, most, shards=(), held_as=jnp.bfloat16):
    gain = shard_levels(key, extent, shards, -0.22, 0.18) if shards else 1.0
    array = jax.random.normal(key, extent, jnp.float32) * scale * gain
    return jnp.minimum(jnp.maximum(array, -most), most).astype(held_as)


def setup_inputs(seed: int = 0) -> dict:
    key_list = jax.random.split(jax.random.key(seed), 10)
    return {
        "moe_input": bell_draw(key_list[0], (TOKENS, D), 1.0, 6.0, ((0, 32),)),
        "out_grad": bell_draw(key_list[1], (TOKENS, D), 0.25, 1.5, ((0, 32),)),
        "context": bell_draw(key_list[2], (TOKENS, QDIM), 0.02, 0.119628906, ((0, 4), (1, 8))),
        "gate_scale": jnp.clip(jnp.exp(math.log(1.0) - 1.609438 * jax.random.uniform(key_list[3], (EXPERTS, CAP), jnp.float32) ** shard_levels(key_list[3], (EXPERTS, CAP), ((0, 32),), -0.2, 0.2)), 0.2, 1.0),
        "selected": draw_selected(jax.random.fold_in(key_list[9], 71), 0),
        "w_gate": bell_draw(key_list[5], (EXPERTS, D, FF), D ** -0.5, 0.125, ((0, 32),)),
        "w_up": bell_draw(key_list[6], (EXPERTS, D, FF), D ** -0.5, 0.125, ((0, 32),)),
        "w_down": bell_draw(key_list[7], (EXPERTS, FF, D), FF ** -0.5, 0.21875, ((0, 32),)),
        "w_out": bell_draw(key_list[8], (QDIM, D), QDIM ** -0.5, 0.09375, ((0, 8),)),
    }


def expert_backward(rows_in, rows_grad, scales, gate_w, up_w, down_w):
    gate_pre = jnp.dot(rows_in, gate_w, preferred_element_type=jnp.float32)
    up_pre = jnp.dot(rows_in, up_w, preferred_element_type=jnp.float32)
    sig = jax.nn.sigmoid(gate_pre)
    silu = gate_pre * sig
    hidden = (silu * up_pre).astype(jnp.bfloat16)
    scaled = (rows_grad.astype(jnp.float32) * scales[:, None]).astype(jnp.bfloat16)
    outer = (((0,), (0,)), ((), ()))
    inner_dims = (((1,), (1,)), ((), ()))
    grad_down = lax.dot_general(hidden, scaled, outer, preferred_element_type=jnp.float32).astype(jnp.bfloat16)
    back_hidden = lax.dot_general(scaled, down_w, inner_dims, preferred_element_type=jnp.float32)
    back_gate = (back_hidden * up_pre * sig * (1.0 + gate_pre * (1.0 - sig))).astype(jnp.bfloat16)
    back_up = (back_hidden * silu).astype(jnp.bfloat16)
    grad_gate = lax.dot_general(rows_in, back_gate, outer, preferred_element_type=jnp.float32).astype(jnp.bfloat16)
    grad_up = lax.dot_general(rows_in, back_up, outer, preferred_element_type=jnp.float32).astype(jnp.bfloat16)
    row_grad = lax.dot_general(back_gate, gate_w, inner_dims, preferred_element_type=jnp.float32)
    row_grad = row_grad + lax.dot_general(back_up, up_w, inner_dims, preferred_element_type=jnp.float32)
    return grad_gate, grad_up, grad_down, row_grad.astype(jnp.bfloat16)


def reference(moe_input, out_grad, context, gate_scale, selected, w_gate, w_up, w_down, w_out):
    def per_expert(packed):
        rows, scales, gate_w, up_w, down_w = packed
        return expert_backward(moe_input[rows], out_grad[rows], scales, gate_w, up_w, down_w)

    grad_gate, grad_up, grad_down, row_grad = lax.map(per_expert, (selected, gate_scale, w_gate, w_up, w_down))
    row_grad = lax.optimization_barrier(row_grad)
    moe_back = jax.ops.segment_sum(row_grad.reshape(-1, D).astype(jnp.float32), selected.reshape(-1).astype(jnp.int32), num_segments=TOKENS)
    total = (out_grad.astype(jnp.float32) + moe_back).astype(jnp.bfloat16)
    grad_context = lax.dot_general(total, w_out, (((1,), (1,)), ((), ())), preferred_element_type=jnp.float32).astype(jnp.bfloat16)
    grad_out = lax.dot_general(context, total, (((0,), (0,)), ((), ())), preferred_element_type=jnp.float32).astype(jnp.bfloat16)
    return grad_gate, grad_up, grad_down, grad_context, grad_out
```

```python
import functools

import jax
import jax.numpy as jnp
from jax import lax
from jax.experimental import pallas as pl
from jax.experimental.pallas import tpu as pltpu
from jax.sharding import PartitionSpec as P

MESH = pl.DeviceIdType.MESH


def split_inner(inner):
    across = 1
    while (2 * across) * (2 * across) <= inner:
        across *= 2
    return inner // across, across


def place():
    groups = lax.axis_size("grp")
    inner = lax.axis_size("inner")
    nz, ny = split_inner(inner)
    g = lax.axis_index("grp")
    i = lax.axis_index("inner")
    z = i // ny
    y = i % ny
    return groups, nz, ny, g, z, y


def at_plane(k, z, ny):
    return (k // ny, z * ny + k % ny)


def greet(g, z, y, nz, ny, planes):
    me = g * ny + y
    barrier = pltpu.get_barrier_semaphore()

    @pl.when(z > 0)
    def _():
        pl.semaphore_signal(barrier, inc=1, device_id=(g, (z - 1) * ny + y), device_id_type=MESH)

    @pl.when(z < nz - 1)
    def _():
        pl.semaphore_signal(barrier, inc=1, device_id=(g, (z + 1) * ny + y), device_id_type=MESH)

    def one(k, carry):
        peer = lax.rem(me + k, planes)
        pl.semaphore_signal(barrier, inc=1, device_id=at_plane(peer, z, ny), device_id_type=MESH)
        return carry

    lax.fori_loop(1, planes, one, 0)
    beside = jnp.where(z > 0, 1, 0) + jnp.where(z < nz - 1, 1, 0)
    pl.semaphore_wait(barrier, planes - 1 + beside)


def remote(src, dst, send, recv, device):
    return pltpu.make_async_remote_copy(
        src_ref=src, dst_ref=dst, send_sem=send, recv_sem=recv, device_id=device, device_id_type=MESH
    )


def dispatch_kernel(
    chunk, x_ref, pick_ref, place_ref, out_ref, gat, stage, recv,
    up_s, up_r, down_s, down_r, plane_s, plane_r,
):
    groups, nz, ny, g, z, y = place()
    planes = groups * ny
    me = g * ny + y
    rows, width = x_ref.shape[1:]
    slots = stage.shape[1] // planes
    parts = width // chunk
    items = 2 * parts
    above = (g, (z + 1) * ny + y)
    below = (g, (z - 1) * ny + y)
    greet(g, z, y, nz, ny, planes)

    def cols(i):
        return pl.ds(pl.multiple_of((i % parts) * chunk, chunk), chunk)

    def block(i, h):
        return gat.at[i // parts, pl.ds(pl.multiple_of(h * rows, rows), rows), cols(i)]

    def up(i, h, s):
        src = x_ref.at[i // parts, :, cols(i)] if s == 0 else block(i, h)
        return remote(src, block(i, h), up_s.at[i, s], up_r.at[i, s], above)

    def down(i, h, s):
        src = x_ref.at[i // parts, :, cols(i)] if s == 0 else block(i, h)
        return remote(src, block(i, h), down_s.at[i, s], down_r.at[i, s], below)

    def own(i):
        @pl.when(z < nz - 1)
        def _():
            up(i, z, 0).start()

        @pl.when(z > 0)
        def _():
            down(i, z, 0).start()

        here = pl.ds(pl.multiple_of(z * rows, rows), rows)
        gat[i // parts, here, cols(i)] = x_ref[i // parts, :, cols(i)]

    def hops(i):
        for s in range(1, nz):
            @pl.when(z - s >= 0)
            def _():
                up(i, z - s, s - 1).wait_recv()

            if s < nz - 1:
                @pl.when((z - s >= 0) & (z < nz - 1))
                def _():
                    up(i, z - s, s).start()

            @pl.when(z + s < nz)
            def _():
                down(i, z + s, s - 1).wait_recv()

            if s < nz - 1:
                @pl.when((z + s < nz) & (z > 0))
                def _():
                    down(i, z + s, s).start()

    def plane(i, k):
        peer = lax.rem(me + k, planes)
        theirs = pl.ds(pl.multiple_of(peer * slots, slots), slots)
        mine = pl.ds(pl.multiple_of(me * slots, slots), slots)
        return remote(
            stage.at[i // parts, theirs, cols(i)], recv.at[i // parts, mine, cols(i)],
            plane_s.at[i, k - 1], plane_r.at[i, k - 1], at_plane(peer, z, ny),
        )

    def pick(i):
        a = i // parts
        stage[a, :, cols(i)] = jnp.dot(
            pick_ref[...], gat[a, :, cols(i)], preferred_element_type=jnp.float32
        ).astype(jnp.bfloat16)

        def one(k, carry):
            plane(i, k).start()
            return carry

        lax.fori_loop(1, planes, one, 0)
        mine = pl.ds(pl.multiple_of(me * slots, slots), slots)
        recv[a, mine, cols(i)] = stage[a, mine, cols(i)]

    def finish(i):
        a = i // parts

        def one(k, carry):
            plane(i, k).wait_recv()
            return carry

        lax.fori_loop(1, planes, one, 0)
        out_ref[a, :, cols(i)] = jnp.dot(
            place_ref[...], recv[a, :, cols(i)], preferred_element_type=jnp.float32
        ).astype(jnp.bfloat16)

    own(0)
    own(1)

    def step(i, carry):
        @pl.when(i + 2 < items)
        def _():
            own(i + 2)

        hops(i)
        pick(i)

        @pl.when(i > 0)
        def _():
            finish(i - 1)

        return carry

    lax.fori_loop(0, items, step, 0)
    finish(items - 1)

    def drain(i, carry):
        for s in range(nz - 1):
            @pl.when((z - s >= 0) & (z < nz - 1))
            def _():
                up(i, z - s, s).wait_send()

            @pl.when((z + s < nz) & (z > 0))
            def _():
                down(i, z + s, s).wait_send()

        def one(k, c):
            plane(i, k).wait_send()
            return c

        return lax.fori_loop(1, planes, one, carry)

    lax.fori_loop(0, items, drain, 0)


def dispatch(x, picker, placer, nz, planes):
    _, rows, width = x.shape
    taken = placer.shape[1]
    cap = placer.shape[0]
    chunk = width // 4
    items = 2 * (width // chunk)
    dma = pltpu.SemaphoreType.DMA
    vmem = pl.BlockSpec(memory_space=pltpu.VMEM)
    return pl.pallas_call(
        functools.partial(dispatch_kernel, chunk),
        out_shape=jax.ShapeDtypeStruct((2, cap, width), jnp.bfloat16),
        in_specs=[vmem] * 3,
        out_specs=vmem,
        scratch_shapes=[
            pltpu.VMEM((2, nz * rows, width), jnp.bfloat16),
            pltpu.VMEM((2, taken, width), jnp.bfloat16),
            pltpu.VMEM((2, taken, width), jnp.bfloat16),
            dma((items, nz - 1)), dma((items, nz - 1)),
            dma((items, nz - 1)), dma((items, nz - 1)),
            dma((items, planes - 1)), dma((items, planes - 1)),
        ],
        compiler_params=pltpu.CompilerParams(
            collective_id=0, has_side_effects=True, vmem_limit_bytes=48 * 2**20
        ),
    )(x, picker, placer)


def collect_kernel(
    chunk, rg_ref, place_ref, pick_ref, og_ref, piece, stage, recv, part,
    from_down, from_up, to_down, to_up,
    plane_s, plane_r, rd_s, rd_r, ru_s, ru_r, up_s, up_r, down_s, down_r, y_s, y_r,
):
    groups, nz, ny, g, z, y = place()
    planes = groups * ny
    me = g * ny + y
    rows, width = og_ref.shape
    slots = stage.shape[0] // planes
    parts = width // chunk
    above = (g, (z + 1) * ny + y)
    below = (g, (z - 1) * ny + y)
    greet(g, z, y, nz, ny, planes)

    def cols(q):
        return pl.ds(pl.multiple_of(q * chunk, chunk), chunk)

    def line(h):
        return pl.ds(pl.multiple_of(h * rows, rows), rows)

    def plane(q, k):
        peer = lax.rem(me + k, planes)
        theirs = pl.ds(pl.multiple_of(peer * slots, slots), slots)
        mine = pl.ds(pl.multiple_of(me * slots, slots), slots)
        return remote(
            stage.at[theirs, cols(q)], recv.at[mine, cols(q)],
            plane_s.at[q, k - 1], plane_r.at[q, k - 1], at_plane(peer, z, ny),
        )

    def reduce_down(q, h):
        return remote(
            to_down.at[line(h), cols(q)], from_up.at[line(h), cols(q)],
            rd_s.at[q, h], rd_r.at[q, h], below,
        )

    def reduce_up(q, h):
        return remote(
            to_up.at[line(h), cols(q)], from_down.at[line(h), cols(q)],
            ru_s.at[q, h], ru_r.at[q, h], above,
        )

    def block(q, h, side):
        return piece.at[pl.ds(pl.multiple_of((h * ny + side) * rows, rows), rows), cols(q)]

    def up(q, h, s):
        return remote(block(q, h, y), block(q, h, y), up_s.at[q, s], up_r.at[q, s], above)

    def down(q, h, s):
        return remote(block(q, h, y), block(q, h, y), down_s.at[q, s], down_r.at[q, s], below)

    def sideways(q, h, k):
        side = lax.rem(y + k, ny)
        return remote(
            block(q, h, y), block(q, h, y), y_s.at[q, h, k - 1], y_r.at[q, h, k - 1],
            (g, z * ny + side),
        )

    def share(q, h):
        for k in range(1, ny):
            sideways(q, h, k).start()

    def scatter(q):
        stage[:, cols(q)] = jnp.dot(
            place_ref[...], rg_ref[:, cols(q)], preferred_element_type=jnp.float32
        ).astype(jnp.bfloat16)

        def one(k, carry):
            plane(q, k).start()
            return carry

        lax.fori_loop(1, planes, one, 0)
        mine = pl.ds(pl.multiple_of(me * slots, slots), slots)
        recv[mine, cols(q)] = stage[mine, cols(q)]

    def gathered(q):
        def one(k, carry):
            plane(q, k).wait_recv()
            return carry

        lax.fori_loop(1, planes, one, 0)
        part[:, cols(q)] = jnp.dot(
            pick_ref[...], recv[:, cols(q)], preferred_element_type=jnp.float32
        )

    def hop(q, h):
        @pl.when(z == nz - 1 - h)
        def _():
            for far in range(nz - 1 - h):
                total = part[line(far), cols(q)]
                if h > 0:
                    reduce_down(q, far).wait_recv()
                    total = total + from_up[line(far), cols(q)].astype(jnp.float32)
                to_down[line(far), cols(q)] = total.astype(jnp.bfloat16)
                reduce_down(q, far).start()

        @pl.when(z == h)
        def _():
            for far in range(nz - 1, h, -1):
                total = part[line(far), cols(q)]
                if h > 0:
                    reduce_up(q, far).wait_recv()
                    total = total + from_down[line(far), cols(q)].astype(jnp.float32)
                to_up[line(far), cols(q)] = total.astype(jnp.bfloat16)
                reduce_up(q, far).start()

    def total(q):
        here = line(z)

        @pl.when(z < nz - 1)
        def _():
            reduce_down(q, z).wait_recv()
            part[here, cols(q)] += from_up[here, cols(q)].astype(jnp.float32)

        @pl.when(z > 0)
        def _():
            reduce_up(q, z).wait_recv()
            part[here, cols(q)] += from_down[here, cols(q)].astype(jnp.float32)

        mine = pl.ds(pl.multiple_of((z * ny + y) * rows, rows), rows)
        piece[mine, cols(q)] = (
            og_ref[:, cols(q)].astype(jnp.float32) + part[here, cols(q)]
        ).astype(jnp.bfloat16)

        @pl.when(z < nz - 1)
        def _():
            up(q, z, 0).start()

        @pl.when(z > 0)
        def _():
            down(q, z, 0).start()

        share(q, z)

    def forward(q, s):
        @pl.when(z - s >= 0)
        def _():
            up(q, z - s, s - 1).wait_recv()
            if s < nz - 1:
                @pl.when(z < nz - 1)
                def _():
                    up(q, z - s, s).start()
            share(q, z - s)

        @pl.when(z + s < nz)
        def _():
            down(q, z + s, s - 1).wait_recv()
            if s < nz - 1:
                @pl.when(z > 0)
                def _():
                    down(q, z + s, s).start()
            share(q, z + s)

    stages = [scatter, gathered]
    stages += [functools.partial(lambda h, q: hop(q, h), h) for h in range(nz - 1)]
    stages += [total]
    stages += [functools.partial(lambda s, q: forward(q, s), s) for s in range(1, nz)]

    def step(t, carry):
        for k in reversed(range(len(stages))):
            @pl.when((t >= k) & (t - k < parts))
            def _():
                stages[k](t - k)

        return carry

    lax.fori_loop(0, parts + len(stages) - 1, step, 0)

    def drain(q, carry):
        def one(k, c):
            plane(q, k).wait_send()
            return c

        lax.fori_loop(1, planes, one, 0)
        for h in range(nz):
            @pl.when(h < z)
            def _():
                reduce_down(q, h).wait_send()

            @pl.when(h > z)
            def _():
                reduce_up(q, h).wait_send()

            for k in range(1, ny):
                side = lax.rem(y + ny - k, ny)
                remote(
                    block(q, h, y), block(q, h, side), y_s.at[q, h, k - 1],
                    y_r.at[q, h, k - 1], (g, z * ny + side),
                ).wait()
        for s in range(nz - 1):
            @pl.when((z - s >= 0) & (z < nz - 1))
            def _():
                up(q, z - s, s).wait_send()

            @pl.when((z + s < nz) & (z > 0))
            def _():
                down(q, z + s, s).wait_send()

        return carry

    lax.fori_loop(0, parts, drain, 0)


def collect(row_grad, placer, picker, out_grad, nz, ny, planes):
    rows, width = out_grad.shape
    taken = placer.shape[0]
    chunk = width // 4
    parts = width // chunk
    dma = pltpu.SemaphoreType.DMA
    vmem = pl.BlockSpec(memory_space=pltpu.VMEM)
    line = (nz * rows, width)
    return pl.pallas_call(
        functools.partial(collect_kernel, chunk),
        out_shape=jax.ShapeDtypeStruct((nz * ny * rows, width), jnp.bfloat16),
        in_specs=[vmem] * 4,
        out_specs=vmem,
        scratch_shapes=[
            pltpu.VMEM((taken, width), jnp.bfloat16),
            pltpu.VMEM((taken, width), jnp.bfloat16),
            pltpu.VMEM(line, jnp.float32),
            pltpu.VMEM(line, jnp.bfloat16),
            pltpu.VMEM(line, jnp.bfloat16),
            pltpu.VMEM(line, jnp.bfloat16),
            pltpu.VMEM(line, jnp.bfloat16),
            dma((parts, planes - 1)), dma((parts, planes - 1)),
            dma((parts, nz)), dma((parts, nz)),
            dma((parts, nz)), dma((parts, nz)),
            dma((parts, nz - 1)), dma((parts, nz - 1)),
            dma((parts, nz - 1)), dma((parts, nz - 1)),
            dma((parts, nz, ny - 1)), dma((parts, nz, ny - 1)),
        ],
        compiler_params=pltpu.CompilerParams(
            collective_id=1, has_side_effects=True, vmem_limit_bytes=48 * 2**20
        ),
    )(row_grad, placer, picker, out_grad)


def expert_backward(rows_in, rows_grad, scales, gate_w, up_w, down_w):
    gate_pre = jnp.dot(rows_in, gate_w, preferred_element_type=jnp.float32)
    up_pre = jnp.dot(rows_in, up_w, preferred_element_type=jnp.float32)
    sig = jax.nn.sigmoid(gate_pre)
    silu = gate_pre * sig
    hidden = (silu * up_pre).astype(jnp.bfloat16)
    scaled = (rows_grad.astype(jnp.float32) * scales[:, None]).astype(jnp.bfloat16)
    outer = (((0,), (0,)), ((), ()))
    inner_dims = (((1,), (1,)), ((), ()))
    back_hidden = lax.dot_general(scaled, down_w, inner_dims, preferred_element_type=jnp.float32)
    back_gate = (back_hidden * up_pre * sig * (1.0 + gate_pre * (1.0 - sig))).astype(jnp.bfloat16)
    back_up = (back_hidden * silu).astype(jnp.bfloat16)
    row_grad = lax.dot_general(back_gate, gate_w, inner_dims, preferred_element_type=jnp.float32)
    row_grad = row_grad + lax.dot_general(
        back_up, up_w, inner_dims, preferred_element_type=jnp.float32
    )
    grad_down = lax.dot_general(hidden, scaled, outer, preferred_element_type=jnp.float32).astype(
        jnp.bfloat16
    )
    grad_gate = lax.dot_general(
        rows_in, back_gate, outer, preferred_element_type=jnp.float32
    ).astype(jnp.bfloat16)
    grad_up = lax.dot_general(rows_in, back_up, outer, preferred_element_type=jnp.float32).astype(
        jnp.bfloat16
    )
    return (grad_gate, grad_up, grad_down, row_grad.astype(jnp.bfloat16))


def tables(selected, rows, most):
    groups, nz, ny, g, z, y = place()
    inner = nz * ny
    planes = groups * ny
    cap = selected.shape[1]
    me = g * ny + y
    experts = selected.reshape(groups, nz, ny, cap)
    experts = lax.dynamic_index_in_dim(experts, z, 1, keepdims=False).reshape(planes, cap)
    owner = experts // rows
    owner_z = (owner % inner) // ny
    owner_p = (owner // inner) * ny + owner % ny
    slot_range = jnp.arange(cap, dtype=jnp.int32)
    earlier = (owner[:, :, None] == owner[:, None, :]) & (
        slot_range[None, :, None] > slot_range[None, None, :]
    )
    ranking = jnp.sum(earlier.astype(jnp.int32), axis=2)
    slots = nz * most
    slot = owner_z * most + ranking
    token = owner_z * rows + experts % rows
    hit = (owner_p == me)[:, :, None] & (
        slot[:, :, None] == jnp.arange(slots, dtype=jnp.int32)[None, None, :]
    )
    table = jnp.sum(jnp.where(hit, token[:, :, None] + 1, 0), axis=1).reshape(-1)
    token_ids = jnp.arange(nz * rows, dtype=jnp.int32) + 1
    picker = (table[:, None] == token_ids[None, :]).astype(jnp.bfloat16)
    position = lax.dynamic_index_in_dim(owner_p * slots + slot, me, 0, keepdims=False)
    arrival = jnp.arange(planes * slots, dtype=jnp.int32)
    placer = (position[:, None] == arrival[None, :]).astype(jnp.bfloat16)
    return picker, placer


def body(moe_input, out_grad, context, gate_scale, selected, w_gate, w_up, w_down, w_out):
    groups = lax.axis_size("grp")
    inner_count = lax.axis_size("inner")
    devices = groups * inner_count
    nz, ny = split_inner(inner_count)
    planes = groups * ny
    tok_rows, width = moe_input.shape
    capacity = selected.shape[1]
    most = max(4, (2 * capacity + devices - 1) // devices)
    picker, placer = tables(selected, tok_rows, most)
    rows = dispatch(jnp.stack([moe_input, out_grad]), picker, placer, nz, planes)
    grad_gate, grad_up, grad_down, row_grad = expert_backward(
        rows[0], rows[1], gate_scale[0], w_gate[0], w_up[0], w_down[0]
    )
    piece = collect(row_grad, placer.T, picker.T, out_grad, nz, ny, planes)
    grad_ctx = lax.dot_general(
        piece, w_out, (((1,), (1,)), ((), ())), preferred_element_type=jnp.float32
    )
    grad_proj = lax.dot_general(
        context, piece, (((0,), (0,)), ((), ())), preferred_element_type=jnp.float32
    )
    proj_share = lax.psum_scatter(
        grad_proj.astype(jnp.bfloat16), "grp", scatter_dimension=1, tiled=True
    )
    return (
        grad_gate[None],
        grad_up[None],
        grad_down[None],
        grad_ctx.astype(jnp.bfloat16),
        proj_share,
    )


def solution(mesh):
    placed = (
        P(("grp", "inner"), None),
        P(("grp", "inner"), None),
        P("grp", "inner"),
        P(("grp", "inner"), None),
        P(),
        P(("grp", "inner"), None, None),
        P(("grp", "inner"), None, None),
        P(("grp", "inner"), None, None),
        P("inner", None),
    )
    return jax.shard_map(
        body,
        mesh=mesh,
        in_specs=placed,
        out_specs=(
            P(("grp", "inner"), None, None),
            P(("grp", "inner"), None, None),
            P(("grp", "inner"), None, None),
            P("grp", "inner"),
            P("inner", "grp"),
        ),
        check_vma=False,
    )
```

```python
import functools

import jax
import jax.numpy as jnp
from jax import lax
from jax.experimental import pallas as pl
from jax.experimental.pallas import tpu as pltpu
from jax.sharding import PartitionSpec as P

MESH = pl.DeviceIdType.MESH


def split_inner(inner):
    across = 1
    while (2 * across) * (2 * across) <= inner:
        across *= 2
    return inner // across, across


def place():
    groups = lax.axis_size("grp")
    inner = lax.axis_size("inner")
    nz, ny = split_inner(inner)
    g = lax.axis_index("grp")
    i = lax.axis_index("inner")
    z = i // ny
    y = i % ny
    return groups, nz, ny, g, z, y


def at_plane(k, z, ny):
    return (k // ny, z * ny + k % ny)


def greet(g, z, y, nz, ny, planes):
    me = g * ny + y
    barrier = pltpu.get_barrier_semaphore()

    @pl.when(z > 0)
    def _():
        pl.semaphore_signal(barrier, inc=1, device_id=(g, (z - 1) * ny + y), device_id_type=MESH)

    @pl.when(z < nz - 1)
    def _():
        pl.semaphore_signal(barrier, inc=1, device_id=(g, (z + 1) * ny + y), device_id_type=MESH)

    def one(k, carry):
        peer = lax.rem(me + k, planes)
        pl.semaphore_signal(barrier, inc=1, device_id=at_plane(peer, z, ny), device_id_type=MESH)
        return carry

    lax.fori_loop(1, planes, one, 0)
    beside = jnp.where(z > 0, 1, 0) + jnp.where(z < nz - 1, 1, 0)
    pl.semaphore_wait(barrier, planes - 1 + beside)


def remote(src, dst, send, recv, device):
    return pltpu.make_async_remote_copy(
        src_ref=src, dst_ref=dst, send_sem=send, recv_sem=recv, device_id=device, device_id_type=MESH
    )


def dispatch_kernel(
    chunk, x_ref, pick_ref, place_ref, out_ref, gat, stage, recv,
    up_s, up_r, down_s, down_r, plane_s, plane_r,
):
    groups, nz, ny, g, z, y = place()
    planes = groups * ny
    me = g * ny + y
    rows, width = x_ref.shape[1:]
    slots = stage.shape[1] // planes
    parts = width // chunk
    items = 2 * parts
    above = (g, (z + 1) * ny + y)
    below = (g, (z - 1) * ny + y)
    greet(g, z, y, nz, ny, planes)

    def cols(i):
        return pl.ds(pl.multiple_of((i % parts) * chunk, chunk), chunk)

    def block(i, h):
        return gat.at[i // parts, pl.ds(pl.multiple_of(h * rows, rows), rows), cols(i)]

    def up(i, h, s):
        src = x_ref.at[i // parts, :, cols(i)] if s == 0 else block(i, h)
        return remote(src, block(i, h), up_s.at[i, s], up_r.at[i, s], above)

    def down(i, h, s):
        src = x_ref.at[i // parts, :, cols(i)] if s == 0 else block(i, h)
        return remote(src, block(i, h), down_s.at[i, s], down_r.at[i, s], below)

    def own(i):
        @pl.when(z < nz - 1)
        def _():
            up(i, z, 0).start()

        @pl.when(z > 0)
        def _():
            down(i, z, 0).start()

        here = pl.ds(pl.multiple_of(z * rows, rows), rows)
        gat[i // parts, here, cols(i)] = x_ref[i // parts, :, cols(i)]

    def hops(i):
        for s in range(1, nz):
            @pl.when(z - s >= 0)
            def _():
                up(i, z - s, s - 1).wait_recv()

            if s < nz - 1:
                @pl.when((z - s >= 0) & (z < nz - 1))
                def _():
                    up(i, z - s, s).start()

            @pl.when(z + s < nz)
            def _():
                down(i, z + s, s - 1).wait_recv()

            if s < nz - 1:
                @pl.when((z + s < nz) & (z > 0))
                def _():
                    down(i, z + s, s).start()

    def plane(i, k):
        peer = lax.rem(me + k, planes)
        theirs = pl.ds(pl.multiple_of(peer * slots, slots), slots)
        mine = pl.ds(pl.multiple_of(me * slots, slots), slots)
        return remote(
            stage.at[i // parts, theirs, cols(i)], recv.at[i // parts, mine, cols(i)],
            plane_s.at[i, k - 1], plane_r.at[i, k - 1], at_plane(peer, z, ny),
        )

    def pick(i):
        a = i // parts
        stage[a, :, cols(i)] = jnp.dot(
            pick_ref[...], gat[a, :, cols(i)], preferred_element_type=jnp.float32
        ).astype(jnp.bfloat16)

        def one(k, carry):
            plane(i, k).start()
            return carry

        lax.fori_loop(1, planes, one, 0)
        mine = pl.ds(pl.multiple_of(me * slots, slots), slots)
        recv[a, mine, cols(i)] = stage[a, mine, cols(i)]

    def finish(i):
        a = i // parts

        def one(k, carry):
            plane(i, k).wait_recv()
            return carry

        lax.fori_loop(1, planes, one, 0)
        out_ref[a, :, cols(i)] = jnp.dot(
            place_ref[...], recv[a, :, cols(i)], preferred_element_type=jnp.float32
        ).astype(jnp.bfloat16)

    own(0)
    own(1)

    def step(i, carry):
        @pl.when(i + 2 < items)
        def _():
            own(i + 2)

        hops(i)
        pick(i)

        @pl.when(i > 0)
        def _():
            finish(i - 1)

        return carry

    lax.fori_loop(0, items, step, 0)
    finish(items - 1)

    def drain(i, carry):
        for s in range(nz - 1):
            @pl.when((z - s >= 0) & (z < nz - 1))
            def _():
                up(i, z - s, s).wait_send()

            @pl.when((z + s < nz) & (z > 0))
            def _():
                down(i, z + s, s).wait_send()

        def one(k, c):
            plane(i, k).wait_send()
            return c

        return lax.fori_loop(1, planes, one, carry)

    lax.fori_loop(0, items, drain, 0)


def dispatch(x, picker, placer, nz, planes):
    _, rows, width = x.shape
    taken = placer.shape[1]
    cap = placer.shape[0]
    chunk = width // 8
    items = 2 * (width // chunk)
    dma = pltpu.SemaphoreType.DMA
    vmem = pl.BlockSpec(memory_space=pltpu.VMEM)
    return pl.pallas_call(
        functools.partial(dispatch_kernel, chunk),
        out_shape=jax.ShapeDtypeStruct((2, cap, width), jnp.bfloat16),
        in_specs=[vmem] * 3,
        out_specs=vmem,
        scratch_shapes=[
            pltpu.VMEM((2, nz * rows, width), jnp.bfloat16),
            pltpu.VMEM((2, taken, width), jnp.bfloat16),
            pltpu.VMEM((2, taken, width), jnp.bfloat16),
            dma((items, nz - 1)), dma((items, nz - 1)),
            dma((items, nz - 1)), dma((items, nz - 1)),
            dma((items, planes - 1)), dma((items, planes - 1)),
        ],
        compiler_params=pltpu.CompilerParams(
            collective_id=0, has_side_effects=True, vmem_limit_bytes=48 * 2**20
        ),
    )(x, picker, placer)


def collect_kernel(
    chunk, rg_ref, place_ref, pick_ref, og_ref, piece, stage, recv, part,
    from_down, from_up, to_down, to_up,
    plane_s, plane_r, rd_s, rd_r, ru_s, ru_r, up_s, up_r, down_s, down_r, y_s, y_r,
):
    groups, nz, ny, g, z, y = place()
    planes = groups * ny
    me = g * ny + y
    rows, width = og_ref.shape
    slots = stage.shape[0] // planes
    parts = width // chunk
    above = (g, (z + 1) * ny + y)
    below = (g, (z - 1) * ny + y)
    greet(g, z, y, nz, ny, planes)

    def cols(q):
        return pl.ds(pl.multiple_of(q * chunk, chunk), chunk)

    def line(h):
        return pl.ds(pl.multiple_of(h * rows, rows), rows)

    def plane(q, k):
        peer = lax.rem(me + k, planes)
        theirs = pl.ds(pl.multiple_of(peer * slots, slots), slots)
        mine = pl.ds(pl.multiple_of(me * slots, slots), slots)
        return remote(
            stage.at[theirs, cols(q)], recv.at[mine, cols(q)],
            plane_s.at[q, k - 1], plane_r.at[q, k - 1], at_plane(peer, z, ny),
        )

    def reduce_down(q, h):
        return remote(
            to_down.at[line(h), cols(q)], from_up.at[line(h), cols(q)],
            rd_s.at[q, h], rd_r.at[q, h], below,
        )

    def reduce_up(q, h):
        return remote(
            to_up.at[line(h), cols(q)], from_down.at[line(h), cols(q)],
            ru_s.at[q, h], ru_r.at[q, h], above,
        )

    def block(q, h, side):
        return piece.at[pl.ds(pl.multiple_of((h * ny + side) * rows, rows), rows), cols(q)]

    def up(q, h, s, k=0):
        this = block(q, h, lax.rem(y + k, ny))
        return remote(this, this, up_s.at[q, k, s], up_r.at[q, k, s], above)

    def down(q, h, s, k=0):
        this = block(q, h, lax.rem(y + k, ny))
        return remote(this, this, down_s.at[q, k, s], down_r.at[q, k, s], below)

    def sideways_first(q):
        return q % 4 == 1

    def beside(q, h, k):
        side = lax.rem(y + k, ny)
        return remote(
            block(q, h, y), block(q, h, side), y_s.at[q, h, ny - 1 - k],
            y_r.at[q, h, ny - 1 - k], (g, z * ny + side),
        )

    def leave(q, k):
        @pl.when(z < nz - 1)
        def _():
            up(q, z, 0, k).start()

        @pl.when(z > 0)
        def _():
            down(q, z, 0, k).start()

    def along(q, s, k):
        @pl.when(z - s >= 0)
        def _():
            up(q, z - s, s - 1, k).wait_recv()
            if s < nz - 1:
                @pl.when(z < nz - 1)
                def _():
                    up(q, z - s, s, k).start()
            if k == 0:
                @pl.when(jnp.logical_not(sideways_first(q)))
                def _():
                    share(q, z - s)

        @pl.when(z + s < nz)
        def _():
            down(q, z + s, s - 1, k).wait_recv()
            if s < nz - 1:
                @pl.when(z > 0)
                def _():
                    down(q, z + s, s, k).start()
            if k == 0:
                @pl.when(jnp.logical_not(sideways_first(q)))
                def _():
                    share(q, z + s)

    def sideways(q, h, k):
        side = lax.rem(y + k, ny)
        return remote(
            block(q, h, y), block(q, h, y), y_s.at[q, h, k - 1], y_r.at[q, h, k - 1],
            (g, z * ny + side),
        )

    def share(q, h):
        for k in range(1, ny):
            sideways(q, h, k).start()

    def scatter(q):
        stage[:, cols(q)] = jnp.dot(
            place_ref[...], rg_ref[:, cols(q)], preferred_element_type=jnp.float32
        ).astype(jnp.bfloat16)

        def one(k, carry):
            plane(q, k).start()
            return carry

        lax.fori_loop(1, planes, one, 0)
        mine = pl.ds(pl.multiple_of(me * slots, slots), slots)
        recv[mine, cols(q)] = stage[mine, cols(q)]

    def gathered(q):
        def one(k, carry):
            plane(q, k).wait_recv()
            return carry

        lax.fori_loop(1, planes, one, 0)
        part[:, cols(q)] = jnp.dot(
            pick_ref[...], recv[:, cols(q)], preferred_element_type=jnp.float32
        )

    def hop(q, h):
        @pl.when(z == nz - 1 - h)
        def _():
            for far in range(nz - 1 - h):
                total = part[line(far), cols(q)]
                if h > 0:
                    reduce_down(q, far).wait_recv()
                    total = total + from_up[line(far), cols(q)].astype(jnp.float32)
                to_down[line(far), cols(q)] = total.astype(jnp.bfloat16)
                reduce_down(q, far).start()

        @pl.when(z == h)
        def _():
            for far in range(nz - 1, h, -1):
                total = part[line(far), cols(q)]
                if h > 0:
                    reduce_up(q, far).wait_recv()
                    total = total + from_down[line(far), cols(q)].astype(jnp.float32)
                to_up[line(far), cols(q)] = total.astype(jnp.bfloat16)
                reduce_up(q, far).start()

    def total(q):
        here = line(z)

        @pl.when(z < nz - 1)
        def _():
            reduce_down(q, z).wait_recv()
            part[here, cols(q)] += from_up[here, cols(q)].astype(jnp.float32)

        @pl.when(z > 0)
        def _():
            reduce_up(q, z).wait_recv()
            part[here, cols(q)] += from_down[here, cols(q)].astype(jnp.float32)

        mine = pl.ds(pl.multiple_of((z * ny + y) * rows, rows), rows)
        piece[mine, cols(q)] = (
            og_ref[:, cols(q)].astype(jnp.float32) + part[here, cols(q)]
        ).astype(jnp.bfloat16)

        leave(q, 0)
        share(q, z)

    def forward(q, s):
        if s < nz:
            along(q, s, 0)

        @pl.when(sideways_first(q))
        def _():
            for k in range(1, ny):
                if s == 1:
                    beside(q, z, k).wait_recv()
                    leave(q, k)
                else:
                    along(q, s - 1, k)

    stages = [scatter, gathered]
    stages += [functools.partial(lambda h, q: hop(q, h), h) for h in range(nz - 1)]
    stages += [total]
    stages += [functools.partial(lambda s, q: forward(q, s), s) for s in range(1, nz + 1)]

    def step(t, carry):
        for k in reversed(range(len(stages))):
            @pl.when((t >= k) & (t - k < parts))
            def _():
                stages[k](t - k)

        return carry

    lax.fori_loop(0, parts + len(stages) - 1, step, 0)

    def drain(q, carry):
        def one(k, c):
            plane(q, k).wait_send()
            return c

        lax.fori_loop(1, planes, one, 0)
        for h in range(nz):
            @pl.when(h < z)
            def _():
                reduce_down(q, h).wait_send()

            @pl.when(h > z)
            def _():
                reduce_up(q, h).wait_send()

            shared = jnp.logical_or(h == z, jnp.logical_not(sideways_first(q)))
            for k in range(1, ny):
                @pl.when(shared)
                def _():
                    sideways(q, h, k).wait_send()

                @pl.when(jnp.logical_not(sideways_first(q)))
                def _():
                    beside(q, h, k).wait_recv()
        for s in range(nz - 1):
            for k in range(ny):
                used = sideways_first(q) if k else (z >= 0)

                @pl.when(used & (z - s >= 0) & (z < nz - 1))
                def _():
                    up(q, z - s, s, k).wait_send()

                @pl.when(used & (z + s < nz) & (z > 0))
                def _():
                    down(q, z + s, s, k).wait_send()

        return carry

    lax.fori_loop(0, parts, drain, 0)


def collect(row_grad, placer, picker, out_grad, nz, ny, planes):
    rows, width = out_grad.shape
    taken = placer.shape[0]
    chunk = width // 8
    parts = width // chunk
    dma = pltpu.SemaphoreType.DMA
    vmem = pl.BlockSpec(memory_space=pltpu.VMEM)
    line = (nz * rows, width)
    return pl.pallas_call(
        functools.partial(collect_kernel, chunk),
        out_shape=jax.ShapeDtypeStruct((nz * ny * rows, width), jnp.bfloat16),
        in_specs=[vmem] * 4,
        out_specs=vmem,
        scratch_shapes=[
            pltpu.VMEM((taken, width), jnp.bfloat16),
            pltpu.VMEM((taken, width), jnp.bfloat16),
            pltpu.VMEM(line, jnp.float32),
            pltpu.VMEM(line, jnp.bfloat16),
            pltpu.VMEM(line, jnp.bfloat16),
            pltpu.VMEM(line, jnp.bfloat16),
            pltpu.VMEM(line, jnp.bfloat16),
            dma((parts, planes - 1)), dma((parts, planes - 1)),
            dma((parts, nz)), dma((parts, nz)),
            dma((parts, nz)), dma((parts, nz)),
            dma((parts, ny, nz - 1)), dma((parts, ny, nz - 1)),
            dma((parts, ny, nz - 1)), dma((parts, ny, nz - 1)),
            dma((parts, nz, ny - 1)), dma((parts, nz, ny - 1)),
        ],
        compiler_params=pltpu.CompilerParams(
            collective_id=1, has_side_effects=True, vmem_limit_bytes=48 * 2**20
        ),
    )(row_grad, placer, picker, out_grad)


def expert_backward(rows_in, rows_grad, scales, gate_w, up_w, down_w):
    gate_pre = jnp.dot(rows_in, gate_w, preferred_element_type=jnp.float32)
    up_pre = jnp.dot(rows_in, up_w, preferred_element_type=jnp.float32)
    sig = jax.nn.sigmoid(gate_pre)
    silu = gate_pre * sig
    hidden = (silu * up_pre).astype(jnp.bfloat16)
    scaled = (rows_grad.astype(jnp.float32) * scales[:, None]).astype(jnp.bfloat16)
    outer = (((0,), (0,)), ((), ()))
    inner_dims = (((1,), (1,)), ((), ()))
    back_hidden = lax.dot_general(scaled, down_w, inner_dims, preferred_element_type=jnp.float32)
    back_gate = (back_hidden * up_pre * sig * (1.0 + gate_pre * (1.0 - sig))).astype(jnp.bfloat16)
    back_up = (back_hidden * silu).astype(jnp.bfloat16)
    row_grad = lax.dot_general(back_gate, gate_w, inner_dims, preferred_element_type=jnp.float32)
    row_grad = row_grad + lax.dot_general(
        back_up, up_w, inner_dims, preferred_element_type=jnp.float32
    )
    grad_down = lax.dot_general(hidden, scaled, outer, preferred_element_type=jnp.float32).astype(
        jnp.bfloat16
    )
    grad_gate = lax.dot_general(
        rows_in, back_gate, outer, preferred_element_type=jnp.float32
    ).astype(jnp.bfloat16)
    grad_up = lax.dot_general(rows_in, back_up, outer, preferred_element_type=jnp.float32).astype(
        jnp.bfloat16
    )
    return (grad_gate, grad_up, grad_down, row_grad.astype(jnp.bfloat16))


def tables(selected, rows, most):
    groups, nz, ny, g, z, y = place()
    inner = nz * ny
    planes = groups * ny
    cap = selected.shape[1]
    me = g * ny + y
    experts = selected.reshape(groups, nz, ny, cap)
    experts = lax.dynamic_index_in_dim(experts, z, 1, keepdims=False).reshape(planes, cap)
    owner = experts // rows
    owner_z = (owner % inner) // ny
    owner_p = (owner // inner) * ny + owner % ny
    slot_range = jnp.arange(cap, dtype=jnp.int32)
    earlier = (owner[:, :, None] == owner[:, None, :]) & (
        slot_range[None, :, None] > slot_range[None, None, :]
    )
    ranking = jnp.sum(earlier.astype(jnp.int32), axis=2)
    slots = nz * most
    slot = owner_z * most + ranking
    token = owner_z * rows + experts % rows
    hit = (owner_p == me)[:, :, None] & (
        slot[:, :, None] == jnp.arange(slots, dtype=jnp.int32)[None, None, :]
    )
    table = jnp.sum(jnp.where(hit, token[:, :, None] + 1, 0), axis=1).reshape(-1)
    token_ids = jnp.arange(nz * rows, dtype=jnp.int32) + 1
    picker = (table[:, None] == token_ids[None, :]).astype(jnp.bfloat16)
    position = lax.dynamic_index_in_dim(owner_p * slots + slot, me, 0, keepdims=False)
    arrival = jnp.arange(planes * slots, dtype=jnp.int32)
    placer = (position[:, None] == arrival[None, :]).astype(jnp.bfloat16)
    return picker, placer


def body(moe_input, out_grad, context, gate_scale, selected, w_gate, w_up, w_down, w_out):
    groups = lax.axis_size("grp")
    inner_count = lax.axis_size("inner")
    devices = groups * inner_count
    nz, ny = split_inner(inner_count)
    planes = groups * ny
    tok_rows, width = moe_input.shape
    capacity = selected.shape[1]
    most = max(4, (2 * capacity + devices - 1) // devices)
    picker, placer = tables(selected, tok_rows, most)
    rows = dispatch(jnp.stack([moe_input, out_grad]), picker, placer, nz, planes)
    grad_gate, grad_up, grad_down, row_grad = expert_backward(
        rows[0], rows[1], gate_scale[0], w_gate[0], w_up[0], w_down[0]
    )
    piece = collect(row_grad, placer.T, picker.T, out_grad, nz, ny, planes)
    grad_ctx = lax.dot_general(
        piece, w_out, (((1,), (1,)), ((), ())), preferred_element_type=jnp.float32
    )
    grad_proj = lax.dot_general(
        context, piece, (((0,), (0,)), ((), ())), preferred_element_type=jnp.float32
    )
    proj_share = lax.psum_scatter(
        grad_proj.astype(jnp.bfloat16), "grp", scatter_dimension=1, tiled=True
    )
    return (
        grad_gate[None],
        grad_up[None],
        grad_down[None],
        grad_ctx.astype(jnp.bfloat16),
        proj_share,
    )


def solution(mesh):
    placed = (
        P(("grp", "inner"), None),
        P(("grp", "inner"), None),
        P("grp", "inner"),
        P(("grp", "inner"), None),
        P(),
        P(("grp", "inner"), None, None),
        P(("grp", "inner"), None, None),
        P(("grp", "inner"), None, None),
        P("inner", None),
    )
    return jax.shard_map(
        body,
        mesh=mesh,
        in_specs=placed,
        out_specs=(
            P(("grp", "inner"), None, None),
            P(("grp", "inner"), None, None),
            P(("grp", "inner"), None, None),
            P("grp", "inner"),
            P("inner", "grp"),
        ),
        check_vma=False,
    )
```

```python
import functools

import jax
import jax.numpy as jnp
from jax import lax
from jax.experimental import pallas as pl
from jax.experimental.pallas import tpu as pltpu
from jax.sharding import PartitionSpec as P

MESH = pl.DeviceIdType.MESH


def split_inner(inner):
    across = 1
    while (2 * across) * (2 * across) <= inner:
        across *= 2
    return inner // across, across


def place():
    groups = lax.axis_size("grp")
    inner = lax.axis_size("inner")
    nz, ny = split_inner(inner)
    g = lax.axis_index("grp")
    i = lax.axis_index("inner")
    z = i // ny
    y = i % ny
    return groups, nz, ny, g, z, y


def at_plane(k, z, ny):
    return (k // ny, z * ny + k % ny)


def greet(g, z, y, nz, ny, planes):
    me = g * ny + y
    barrier = pltpu.get_barrier_semaphore()

    @pl.when(z > 0)
    def _():
        pl.semaphore_signal(barrier, inc=1, device_id=(g, (z - 1) * ny + y), device_id_type=MESH)

    @pl.when(z < nz - 1)
    def _():
        pl.semaphore_signal(barrier, inc=1, device_id=(g, (z + 1) * ny + y), device_id_type=MESH)

    def one(k, carry):
        peer = lax.rem(me + k, planes)
        pl.semaphore_signal(barrier, inc=1, device_id=at_plane(peer, z, ny), device_id_type=MESH)
        return carry

    lax.fori_loop(1, planes, one, 0)
    beside = jnp.where(z > 0, 1, 0) + jnp.where(z < nz - 1, 1, 0)
    pl.semaphore_wait(barrier, planes - 1 + beside)


def remote(src, dst, send, recv, device):
    return pltpu.make_async_remote_copy(
        src_ref=src, dst_ref=dst, send_sem=send, recv_sem=recv, device_id=device, device_id_type=MESH
    )


def dispatch_kernel(
    chunk, in_ref, grad_ref, pick_ref, place_ref, out_ref, gat, stage, recv,
    up_s, up_r, down_s, down_r, plane_s, plane_r,
):
    groups, nz, ny, g, z, y = place()
    planes = groups * ny
    me = g * ny + y
    rows, width = in_ref.shape
    slots = stage.shape[1] // planes
    parts = width // chunk
    items = 2 * parts
    above = (g, (z + 1) * ny + y)
    below = (g, (z - 1) * ny + y)
    greet(g, z, y, nz, ny, planes)

    def cols(i):
        return pl.ds(pl.multiple_of((i % parts) * chunk, chunk), chunk)

    def block(i, h):
        return gat.at[i, pl.ds(pl.multiple_of(h * rows, rows), rows)]

    def up(i, h, s):
        return remote(block(i, h), block(i, h), up_s.at[i, s], up_r.at[i, s], above)

    def down(i, h, s):
        return remote(block(i, h), block(i, h), down_s.at[i, s], down_r.at[i, s], below)

    def own(i):
        @pl.when(z < nz - 1)
        def _():
            up(i, z, 0).start()

        @pl.when(z > 0)
        def _():
            down(i, z, 0).start()

    def hops(i):
        for s in range(1, nz):
            @pl.when(z - s >= 0)
            def _():
                up(i, z - s, s - 1).wait_recv()

            if s < nz - 1:
                @pl.when((z - s >= 0) & (z < nz - 1))
                def _():
                    up(i, z - s, s).start()

            @pl.when(z + s < nz)
            def _():
                down(i, z + s, s - 1).wait_recv()

            if s < nz - 1:
                @pl.when((z + s < nz) & (z > 0))
                def _():
                    down(i, z + s, s).start()

    def plane(i, k):
        peer = lax.rem(me + k, planes)
        theirs = pl.ds(pl.multiple_of(peer * slots, slots), slots)
        mine = pl.ds(pl.multiple_of(me * slots, slots), slots)
        return remote(
            stage.at[i, theirs], recv.at[i, mine],
            plane_s.at[i, k - 1], plane_r.at[i, k - 1], at_plane(peer, z, ny),
        )

    def pick(i):
        stage[i] = jnp.dot(
            pick_ref[...], gat[i], preferred_element_type=jnp.float32
        ).astype(jnp.bfloat16)

        def one(k, carry):
            plane(i, k).start()
            return carry

        lax.fori_loop(1, planes, one, 0)
        mine = pl.ds(pl.multiple_of(me * slots, slots), slots)
        recv[i, mine] = stage[i, mine]

    def finish(i):
        a = i // parts

        def one(k, carry):
            plane(i, k).wait_recv()
            return carry

        lax.fori_loop(1, planes, one, 0)
        out_ref[a, :, cols(i)] = jnp.dot(
            place_ref[...], recv[i], preferred_element_type=jnp.float32
        ).astype(jnp.bfloat16)

    here = pl.ds(pl.multiple_of(z * rows, rows), rows)
    for i in range(items):
        ref = in_ref if i < parts else grad_ref
        gat[i, here] = ref[:, (i % parts) * chunk : (i % parts + 1) * chunk]

    own(0)
    own(1)

    def step(i, carry):
        @pl.when(i + 2 < items)
        def _():
            own(i + 2)

        hops(i)
        pick(i)

        @pl.when(i > 0)
        def _():
            finish(i - 1)

        return carry

    lax.fori_loop(0, items, step, 0)
    finish(items - 1)

    def drain(i, carry):
        for s in range(nz - 1):
            @pl.when((z - s >= 0) & (z < nz - 1))
            def _():
                up(i, z - s, s).wait_send()

            @pl.when((z + s < nz) & (z > 0))
            def _():
                down(i, z + s, s).wait_send()

        def one(k, c):
            plane(i, k).wait_send()
            return c

        return lax.fori_loop(1, planes, one, carry)

    lax.fori_loop(0, items, drain, 0)


def dispatch(moe_input, out_grad, picker, placer, nz, planes):
    rows, width = moe_input.shape
    taken = placer.shape[1]
    cap = placer.shape[0]
    chunk = width // 4
    items = 2 * (width // chunk)
    dma = pltpu.SemaphoreType.DMA
    vmem = pl.BlockSpec(memory_space=pltpu.VMEM)
    return pl.pallas_call(
        functools.partial(dispatch_kernel, chunk),
        out_shape=jax.ShapeDtypeStruct((2, cap, width), jnp.bfloat16),
        in_specs=[vmem] * 4,
        out_specs=vmem,
        scratch_shapes=[
            pltpu.VMEM((items, nz * rows, chunk), jnp.bfloat16),
            pltpu.VMEM((items, taken, chunk), jnp.bfloat16),
            pltpu.VMEM((items, taken, chunk), jnp.bfloat16),
            dma((items, nz - 1)), dma((items, nz - 1)),
            dma((items, nz - 1)), dma((items, nz - 1)),
            dma((items, planes - 1)), dma((items, planes - 1)),
        ],
        compiler_params=pltpu.CompilerParams(
            collective_id=0, has_side_effects=True, vmem_limit_bytes=48 * 2**20
        ),
    )(moe_input, out_grad, picker, placer)


def collect_kernel(
    rg_ref, place_ref, pick_ref, og_ref, context_ref, wout_ref, ctx_ref, proj_ref,
    stage, recv, part, piece, ctx, proj, proj_in, from_down, from_up, to_down, to_up,
    plane_s, plane_r, rd_s, rd_r, ru_s, ru_r, up_s, up_r, down_s, down_r, y_s, y_r, proj_s, proj_r,
):
    groups, nz, ny, g, z, y = place()
    planes = groups * ny
    me = g * ny + y
    rows, width = og_ref.shape
    slots = stage.shape[1] // planes
    parts = groups
    chunk = width // parts
    above = (g, (z + 1) * ny + y)
    below = (g, (z - 1) * ny + y)
    greet(g, z, y, nz, ny, planes)

    def owner(q, group):
        return lax.rem(group + q + 1, groups)

    def cols(q, group=g):
        return pl.ds(pl.multiple_of(owner(q, group) * chunk, chunk), chunk)

    def line(h):
        return pl.ds(pl.multiple_of(h * rows, rows), rows)

    def plane(q, k):
        peer = lax.rem(me + k, planes)
        theirs = pl.ds(pl.multiple_of(peer * slots, slots), slots)
        mine = pl.ds(pl.multiple_of(me * slots, slots), slots)
        return remote(
            stage.at[q, theirs], recv.at[q, mine],
            plane_s.at[q, k - 1], plane_r.at[q, k - 1], at_plane(peer, z, ny),
        )

    def reduce_down(q, h):
        return remote(
            to_down.at[q, line(h)], from_up.at[q, line(h)],
            rd_s.at[q, h], rd_r.at[q, h], below,
        )

    def reduce_up(q, h):
        return remote(
            to_up.at[q, line(h)], from_down.at[q, line(h)],
            ru_s.at[q, h], ru_r.at[q, h], above,
        )

    def block(q, h, side):
        return piece.at[q, pl.ds(pl.multiple_of((h * ny + side) * rows, rows), rows)]

    def up(q, h, s, k=0):
        this = block(q, h, lax.rem(y + k, ny))
        return remote(this, this, up_s.at[q, k, s], up_r.at[q, k, s], above)

    def down(q, h, s, k=0):
        this = block(q, h, lax.rem(y + k, ny))
        return remote(this, this, down_s.at[q, k, s], down_r.at[q, k, s], below)

    def sideways_first(q):
        return q % 4 == 1

    def beside(q, h, k):
        side = lax.rem(y + k, ny)
        return remote(
            block(q, h, y), block(q, h, side), y_s.at[q, h, ny - 1 - k],
            y_r.at[q, h, ny - 1 - k], (g, z * ny + side),
        )

    def leave(q, k):
        @pl.when(z < nz - 1)
        def _():
            up(q, z, 0, k).start()

        @pl.when(z > 0)
        def _():
            down(q, z, 0, k).start()

    def along(q, s, k):
        @pl.when(z - s >= 0)
        def _():
            up(q, z - s, s - 1, k).wait_recv()
            if s < nz - 1:
                @pl.when(z < nz - 1)
                def _():
                    up(q, z - s, s, k).start()
            if k == 0:
                @pl.when(jnp.logical_not(sideways_first(q)))
                def _():
                    share(q, z - s)

        @pl.when(z + s < nz)
        def _():
            down(q, z + s, s - 1, k).wait_recv()
            if s < nz - 1:
                @pl.when(z > 0)
                def _():
                    down(q, z + s, s, k).start()
            if k == 0:
                @pl.when(jnp.logical_not(sideways_first(q)))
                def _():
                    share(q, z + s)

    def sideways(q, h, k):
        side = lax.rem(y + k, ny)
        return remote(
            block(q, h, y), block(q, h, y), y_s.at[q, h, k - 1], y_r.at[q, h, k - 1],
            (g, z * ny + side),
        )

    def share(q, h):
        for k in range(1, ny):
            sideways(q, h, k).start()

    def scatter(q):
        span = ny * slots
        for group in range(groups):
            stage[q, group * span : (group + 1) * span] = jnp.dot(
                place_ref[group * span : (group + 1) * span, :],
                rg_ref[:, cols(q, group)],
                preferred_element_type=jnp.float32,
            ).astype(jnp.bfloat16)

        def one(k, carry):
            plane(q, k).start()
            return carry

        lax.fori_loop(1, planes, one, 0)
        mine = pl.ds(pl.multiple_of(me * slots, slots), slots)
        recv[q, mine] = stage[q, mine]

    def gathered(q):
        def one(k, carry):
            plane(q, k).wait_recv()
            return carry

        lax.fori_loop(1, planes, one, 0)
        part[q] = jnp.dot(
            pick_ref[...], recv[q], preferred_element_type=jnp.float32
        )

    def hop(q, h):
        @pl.when(z == nz - 1 - h)
        def _():
            for far in range(nz - 1 - h):
                total = part[q, line(far)]
                if h > 0:
                    reduce_down(q, far).wait_recv()
                    total = total + from_up[q, line(far)].astype(jnp.float32)
                to_down[q, line(far)] = total.astype(jnp.bfloat16)
                reduce_down(q, far).start()

        @pl.when(z == h)
        def _():
            for far in range(nz - 1, h, -1):
                total = part[q, line(far)]
                if h > 0:
                    reduce_up(q, far).wait_recv()
                    total = total + from_down[q, line(far)].astype(jnp.float32)
                to_up[q, line(far)] = total.astype(jnp.bfloat16)
                reduce_up(q, far).start()

    def total(q):
        here = line(z)

        @pl.when(z < nz - 1)
        def _():
            reduce_down(q, z).wait_recv()
            part[q, here] += from_up[q, here].astype(jnp.float32)

        @pl.when(z > 0)
        def _():
            reduce_up(q, z).wait_recv()
            part[q, here] += from_down[q, here].astype(jnp.float32)

        mine = pl.ds(pl.multiple_of((z * ny + y) * rows, rows), rows)
        piece[q, mine] = (
            og_ref[:, cols(q)].astype(jnp.float32) + part[q, here]
        ).astype(jnp.bfloat16)

        leave(q, 0)
        share(q, z)

    def forward(q, s):
        if s < nz:
            along(q, s, 0)

        @pl.when(sideways_first(q))
        def _():
            for k in range(1, ny):
                if s == 1:
                    beside(q, z, k).wait_recv()
                    leave(q, k)
                else:
                    along(q, s - 1, k)

    def project(q):
        @pl.when(jnp.logical_not(sideways_first(q)))
        def _():
            for h in range(nz):
                for k in range(1, ny):
                    beside(q, h, k).wait_recv()

        totals = piece[q]
        term = lax.dot_general(
            totals, wout_ref[:, cols(q)], (((1,), (1,)), ((), ())),
            preferred_element_type=jnp.float32,
        )

        @pl.when(q == 0)
        def _():
            ctx[...] = term

        @pl.when(q > 0)
        def _():
            ctx[...] += term

        share_of = lax.dot_general(
            context_ref[...], totals, (((0,), (0,)), ((), ())),
            preferred_element_type=jnp.float32,
        )

        @pl.when(q < parts - 1)
        def _():
            proj[q] = share_of.astype(jnp.bfloat16)
            to_owner(q).start()

        @pl.when(q == parts - 1)
        def _():
            acc = share_of
            for other in range(parts - 1):
                to_owner(other).wait_recv()
                acc = acc + proj_in[other].astype(jnp.float32)
            proj_ref[...] = acc.astype(jnp.bfloat16)
            ctx_ref[...] = ctx[...].astype(jnp.bfloat16)

    def to_owner(q):
        return remote(
            proj.at[q], proj_in.at[q], proj_s.at[q], proj_r.at[q],
            (owner(q, g), z * ny + y),
        )

    stages = [scatter, gathered]
    stages += [functools.partial(lambda h, q: hop(q, h), h) for h in range(nz - 1)]
    stages += [total]
    stages += [functools.partial(lambda s, q: forward(q, s), s) for s in range(1, nz + 1)]
    stages += [project]

    last = len(stages) - 1

    def step(t, carry):
        for k in [*reversed(range(last)), last]:
            @pl.when((t >= k) & (t - k < parts))
            def _():
                stages[k](t - k)

        return carry

    lax.fori_loop(0, parts + last, step, 0)

    def drain(q, carry):
        def one(k, c):
            plane(q, k).wait_send()
            return c

        lax.fori_loop(1, planes, one, 0)
        for h in range(nz):
            @pl.when(h < z)
            def _():
                reduce_down(q, h).wait_send()

            @pl.when(h > z)
            def _():
                reduce_up(q, h).wait_send()

            shared = jnp.logical_or(h == z, jnp.logical_not(sideways_first(q)))
            for k in range(1, ny):
                @pl.when(shared)
                def _():
                    sideways(q, h, k).wait_send()
        for s in range(nz - 1):
            for k in range(ny):
                used = sideways_first(q) if k else (z >= 0)

                @pl.when(used & (z - s >= 0) & (z < nz - 1))
                def _():
                    up(q, z - s, s, k).wait_send()

                @pl.when(used & (z + s < nz) & (z > 0))
                def _():
                    down(q, z + s, s, k).wait_send()

        @pl.when(q < parts - 1)
        def _():
            to_owner(q).wait_send()

        return carry

    lax.fori_loop(0, parts, drain, 0)


def collect(row_grad, placer, picker, out_grad, context, w_out, groups, nz, ny):
    rows, width = out_grad.shape
    features = w_out.shape[0]
    taken = placer.shape[0]
    planes = groups * ny
    parts = groups
    chunk = width // parts
    tokens = nz * ny * rows
    dma = pltpu.SemaphoreType.DMA
    vmem = pl.BlockSpec(memory_space=pltpu.VMEM)
    line = (parts, nz * rows, chunk)
    return pl.pallas_call(
        collect_kernel,
        out_shape=(
            jax.ShapeDtypeStruct((tokens, features), jnp.bfloat16),
            jax.ShapeDtypeStruct((features, chunk), jnp.bfloat16),
        ),
        in_specs=[vmem] * 6,
        out_specs=(vmem, vmem),
        scratch_shapes=[
            pltpu.VMEM((parts, taken, chunk), jnp.bfloat16),
            pltpu.VMEM((parts, taken, chunk), jnp.bfloat16),
            pltpu.VMEM(line, jnp.float32),
            pltpu.VMEM((parts, tokens, chunk), jnp.bfloat16),
            pltpu.VMEM((tokens, features), jnp.float32),
            pltpu.VMEM((parts - 1, features, chunk), jnp.bfloat16),
            pltpu.VMEM((parts - 1, features, chunk), jnp.bfloat16),
            pltpu.VMEM(line, jnp.bfloat16),
            pltpu.VMEM(line, jnp.bfloat16),
            pltpu.VMEM(line, jnp.bfloat16),
            pltpu.VMEM(line, jnp.bfloat16),
            dma((parts, planes - 1)), dma((parts, planes - 1)),
            dma((parts, nz)), dma((parts, nz)),
            dma((parts, nz)), dma((parts, nz)),
            dma((parts, ny, nz - 1)), dma((parts, ny, nz - 1)),
            dma((parts, ny, nz - 1)), dma((parts, ny, nz - 1)),
            dma((parts, nz, ny - 1)), dma((parts, nz, ny - 1)),
            dma((parts - 1,)), dma((parts - 1,)),
        ],
        compiler_params=pltpu.CompilerParams(
            collective_id=1, has_side_effects=True, vmem_limit_bytes=50 * 2**20
        ),
    )(row_grad, placer, picker, out_grad, context, w_out)


def expert_backward(rows_in, rows_grad, scales, gate_w, up_w, down_w):
    gate_pre = jnp.dot(rows_in, gate_w, preferred_element_type=jnp.float32)
    up_pre = jnp.dot(rows_in, up_w, preferred_element_type=jnp.float32)
    sig = jax.nn.sigmoid(gate_pre)
    silu = gate_pre * sig
    hidden = (silu * up_pre).astype(jnp.bfloat16)
    scaled = (rows_grad.astype(jnp.float32) * scales[:, None]).astype(jnp.bfloat16)
    outer = (((0,), (0,)), ((), ()))
    inner_dims = (((1,), (1,)), ((), ()))
    back_hidden = lax.dot_general(scaled, down_w, inner_dims, preferred_element_type=jnp.float32)
    back_gate = (back_hidden * up_pre * sig * (1.0 + gate_pre * (1.0 - sig))).astype(jnp.bfloat16)
    back_up = (back_hidden * silu).astype(jnp.bfloat16)
    row_grad = lax.dot_general(back_gate, gate_w, inner_dims, preferred_element_type=jnp.float32)
    row_grad = row_grad + lax.dot_general(
        back_up, up_w, inner_dims, preferred_element_type=jnp.float32
    )
    grad_down = lax.dot_general(hidden, scaled, outer, preferred_element_type=jnp.float32).astype(
        jnp.bfloat16
    )
    grad_gate = lax.dot_general(
        rows_in, back_gate, outer, preferred_element_type=jnp.float32
    ).astype(jnp.bfloat16)
    grad_up = lax.dot_general(rows_in, back_up, outer, preferred_element_type=jnp.float32).astype(
        jnp.bfloat16
    )
    return (grad_gate, grad_up, grad_down, row_grad.astype(jnp.bfloat16))


def tables(selected, rows, most):
    groups, nz, ny, g, z, y = place()
    inner = nz * ny
    planes = groups * ny
    cap = selected.shape[1]
    me = g * ny + y
    experts = selected.reshape(groups, nz, ny, cap)
    experts = lax.dynamic_index_in_dim(experts, z, 1, keepdims=False).reshape(planes, cap)
    owner = experts // rows
    owner_z = (owner % inner) // ny
    owner_p = (owner // inner) * ny + owner % ny
    slot_range = jnp.arange(cap, dtype=jnp.int32)
    earlier = (owner[:, :, None] == owner[:, None, :]) & (
        slot_range[None, :, None] > slot_range[None, None, :]
    )
    ranking = jnp.sum(earlier.astype(jnp.int32), axis=2)
    slots = nz * most
    slot = owner_z * most + ranking
    token = owner_z * rows + experts % rows
    hit = (owner_p == me)[:, :, None] & (
        slot[:, :, None] == jnp.arange(slots, dtype=jnp.int32)[None, None, :]
    )
    table = jnp.sum(jnp.where(hit, token[:, :, None] + 1, 0), axis=1).reshape(-1)
    token_ids = jnp.arange(nz * rows, dtype=jnp.int32) + 1
    picker = (table[:, None] == token_ids[None, :]).astype(jnp.bfloat16)
    position = lax.dynamic_index_in_dim(owner_p * slots + slot, me, 0, keepdims=False)
    arrival = jnp.arange(planes * slots, dtype=jnp.int32)
    placer = (position[:, None] == arrival[None, :]).astype(jnp.bfloat16)
    return picker, placer


def body(moe_input, out_grad, context, gate_scale, selected, w_gate, w_up, w_down, w_out):
    groups = lax.axis_size("grp")
    inner_count = lax.axis_size("inner")
    devices = groups * inner_count
    nz, ny = split_inner(inner_count)
    planes = groups * ny
    tok_rows, width = moe_input.shape
    capacity = selected.shape[1]
    most = max(4, (2 * capacity + devices - 1) // devices)
    picker, placer = tables(selected, tok_rows, most)
    rows = dispatch(moe_input, out_grad, picker, placer, nz, planes)
    grad_gate, grad_up, grad_down, row_grad = expert_backward(
        rows[0], rows[1], gate_scale[0], w_gate[0], w_up[0], w_down[0]
    )
    grad_ctx, grad_proj = collect(
        row_grad, placer.T, picker.T, out_grad, context, w_out, groups, nz, ny
    )
    return (
        grad_gate[None],
        grad_up[None],
        grad_down[None],
        grad_ctx,
        grad_proj,
    )


def solution(mesh):
    placed = (
        P(("grp", "inner"), None),
        P(("grp", "inner"), None),
        P("grp", "inner"),
        P(("grp", "inner"), None),
        P(),
        P(("grp", "inner"), None, None),
        P(("grp", "inner"), None, None),
        P(("grp", "inner"), None, None),
        P("inner", None),
    )
    return jax.shard_map(
        body,
        mesh=mesh,
        in_specs=placed,
        out_specs=(
            P(("grp", "inner"), None, None),
            P(("grp", "inner"), None, None),
            P(("grp", "inner"), None, None),
            P("grp", "inner"),
            P("inner", "grp"),
        ),
        check_vma=False,
    )
```

```python
import functools

import jax
import jax.numpy as jnp
from jax import lax
from jax.experimental import pallas as pl
from jax.experimental.pallas import tpu as pltpu
from jax.sharding import PartitionSpec as P

MESH = pl.DeviceIdType.MESH


def split_inner(inner):
    across = 1
    while (2 * across) * (2 * across) <= inner:
        across *= 2
    return inner // across, across


def place():
    groups = lax.axis_size("grp")
    inner = lax.axis_size("inner")
    nz, ny = split_inner(inner)
    g = lax.axis_index("grp")
    i = lax.axis_index("inner")
    z = i // ny
    y = i % ny
    return groups, nz, ny, g, z, y


def at_plane(k, z, ny):
    return (k // ny, z * ny + k % ny)


def greet(g, z, y, nz, ny, planes):
    me = g * ny + y
    barrier = pltpu.get_barrier_semaphore()

    for k in range(1, nz):
        height = lax.rem(z + k, nz)
        pl.semaphore_signal(barrier, inc=1, device_id=(g, height * ny + y), device_id_type=MESH)

    def one(k, carry):
        peer = lax.rem(me + k, planes)
        pl.semaphore_signal(barrier, inc=1, device_id=at_plane(peer, z, ny), device_id_type=MESH)
        return carry

    lax.fori_loop(1, planes, one, 0)
    pl.semaphore_wait(barrier, planes - 1 + nz - 1)


def remote(src, dst, send, recv, device):
    return pltpu.make_async_remote_copy(
        src_ref=src, dst_ref=dst, send_sem=send, recv_sem=recv, device_id=device, device_id_type=MESH
    )


def dispatch_kernel(
    chunk, in_ref, grad_ref, pick_ref, place_ref, out_ref, gat, stage, recv,
    up_s, up_r, down_s, down_r, plane_s, plane_r, own_s,
):
    groups, nz, ny, g, z, y = place()
    planes = groups * ny
    me = g * ny + y
    rows, width = in_ref.shape
    slots = stage.shape[1] // planes
    parts = width // chunk
    items = 2 * parts
    ahead = 3
    above = (g, (z + 1) * ny + y)
    below = (g, (z - 1) * ny + y)
    here = pl.ds(pl.multiple_of(z * rows, rows), rows)

    def fetch(i):
        ref = in_ref if i < parts else grad_ref
        taken = ref.at[:, pl.ds((i % parts) * chunk, chunk)]
        return pltpu.make_async_copy(taken, gat.at[i, here], own_s.at[i])

    for i in range(items):
        fetch(i).start()
    greet(g, z, y, nz, ny, planes)

    def cols(i):
        return pl.ds(pl.multiple_of((i % parts) * chunk, chunk), chunk)

    def block(i, h):
        return gat.at[i, pl.ds(pl.multiple_of(h * rows, rows), rows)]

    def up(i, h, s):
        return remote(block(i, h), block(i, h), up_s.at[i, s], up_r.at[i, s], above)

    def down(i, h, s):
        return remote(block(i, h), block(i, h), down_s.at[i, s], down_r.at[i, s], below)

    def own(i):
        @pl.when(z < nz - 1)
        def _():
            up(i, z, 0).start()

        @pl.when(z > 0)
        def _():
            down(i, z, 0).start()

    def hops(i):
        for s in range(1, nz):
            @pl.when(z - s >= 0)
            def _():
                up(i, z - s, s - 1).wait_recv()

            if s < nz - 1:
                @pl.when((z - s >= 0) & (z < nz - 1))
                def _():
                    up(i, z - s, s).start()

            @pl.when(z + s < nz)
            def _():
                down(i, z + s, s - 1).wait_recv()

            if s < nz - 1:
                @pl.when((z + s < nz) & (z > 0))
                def _():
                    down(i, z + s, s).start()

    def plane(i, k):
        peer = lax.rem(me + k, planes)
        theirs = pl.ds(pl.multiple_of(peer * slots, slots), slots)
        mine = pl.ds(pl.multiple_of(me * slots, slots), slots)
        return remote(
            stage.at[i, theirs], recv.at[i, mine],
            plane_s.at[i, k - 1], plane_r.at[i, k - 1], at_plane(peer, z, ny),
        )

    def pick(i):
        stage[i] = jnp.dot(
            pick_ref[...], gat[i], preferred_element_type=jnp.float32
        ).astype(jnp.bfloat16)

        def one(k, carry):
            plane(i, k).start()
            return carry

        lax.fori_loop(1, planes, one, 0)
        mine = pl.ds(pl.multiple_of(me * slots, slots), slots)
        recv[i, mine] = stage[i, mine]

    def finish(i):
        a = i // parts

        def one(k, carry):
            plane(i, k).wait_recv()
            return carry

        lax.fori_loop(1, planes, one, 0)
        out_ref[a, :, cols(i)] = jnp.dot(
            place_ref[...], recv[i], preferred_element_type=jnp.float32
        ).astype(jnp.bfloat16)

    for i in range(items):
        fetch(i).wait()

    for i in range(ahead):
        own(i)

    def step(i, carry):
        @pl.when(i + ahead < items)
        def _():
            own(i + ahead)

        hops(i)
        pick(i)

        @pl.when(i > 1)
        def _():
            finish(i - 2)

        return carry

    lax.fori_loop(0, items, step, 0)
    finish(items - 2)
    finish(items - 1)

    def drain(i, carry):
        for s in range(nz - 1):
            @pl.when((z - s >= 0) & (z < nz - 1))
            def _():
                up(i, z - s, s).wait_send()

            @pl.when((z + s < nz) & (z > 0))
            def _():
                down(i, z + s, s).wait_send()

        def one(k, c):
            plane(i, k).wait_send()
            return c

        return lax.fori_loop(1, planes, one, carry)

    lax.fori_loop(0, items, drain, 0)


def dispatch(moe_input, out_grad, picker, placer, nz, planes):
    rows, width = moe_input.shape
    taken = placer.shape[1]
    cap = placer.shape[0]
    chunk = width // 4
    items = 2 * (width // chunk)
    dma = pltpu.SemaphoreType.DMA
    vmem = pl.BlockSpec(memory_space=pltpu.VMEM)
    return pl.pallas_call(
        functools.partial(dispatch_kernel, chunk),
        out_shape=jax.ShapeDtypeStruct((2, cap, width), jnp.bfloat16),
        in_specs=[pl.BlockSpec(memory_space=pl.ANY)] * 2 + [vmem] * 2,
        out_specs=vmem,
        scratch_shapes=[
            pltpu.VMEM((items, nz * rows, chunk), jnp.bfloat16),
            pltpu.VMEM((items, taken, chunk), jnp.bfloat16),
            pltpu.VMEM((items, taken, chunk), jnp.bfloat16),
            dma((items, nz - 1)), dma((items, nz - 1)),
            dma((items, nz - 1)), dma((items, nz - 1)),
            dma((items, planes - 1)), dma((items, planes - 1)),
            dma((items,)),
        ],
        compiler_params=pltpu.CompilerParams(
            collective_id=0, has_side_effects=True, vmem_limit_bytes=24 * 2**20
        ),
    )(moe_input, out_grad, picker, placer)


def collect_kernel(
    rg_ref, place_ref, pick_ref, og_ref, context_ref, wout_ref, ctx_ref, proj_ref,
    stage, recv, part, piece, ctx, proj, proj_in, to_line, from_line,
    plane_s, plane_r, sum_s, sum_r, up_s, up_r, down_s, down_r, y_s, y_r, proj_s, proj_r,
):
    groups, nz, ny, g, z, y = place()
    planes = groups * ny
    me = g * ny + y
    rows, width = og_ref.shape
    slots = stage.shape[1] // planes
    parts = groups
    chunk = width // parts
    above = (g, (z + 1) * ny + y)
    below = (g, (z - 1) * ny + y)
    greet(g, z, y, nz, ny, planes)

    def owner(q, group):
        return lax.rem(group + q + 1, groups)

    def cols(q, group=g):
        return pl.ds(pl.multiple_of(owner(q, group) * chunk, chunk), chunk)

    def line(h):
        return pl.ds(pl.multiple_of(h * rows, rows), rows)

    def plane(q, k):
        peer = lax.rem(me + k, planes)
        theirs = pl.ds(pl.multiple_of(peer * slots, slots), slots)
        mine = pl.ds(pl.multiple_of(me * slots, slots), slots)
        return remote(
            stage.at[q, theirs], recv.at[q, mine],
            plane_s.at[q, k - 1], plane_r.at[q, k - 1], at_plane(peer, z, ny),
        )

    def to_height(q, k):
        h = lax.rem(z + k, nz)
        return remote(
            to_line.at[q, line(h)], from_line.at[q, line(z)],
            sum_s.at[q, k - 1], sum_r.at[q, k - 1], (g, h * ny + y),
        )

    def from_height(q, k):
        h = lax.rem(z + k, nz)
        return remote(
            to_line.at[q, line(h)], from_line.at[q, line(h)],
            sum_s.at[q, nz - 1 - k], sum_r.at[q, nz - 1 - k], (g, h * ny + y),
        )

    def block(q, h, side):
        return piece.at[q, pl.ds(pl.multiple_of((h * ny + side) * rows, rows), rows)]

    def up(q, h, s):
        return remote(block(q, h, y), block(q, h, y), up_s.at[q, s], up_r.at[q, s], above)

    def down(q, h, s):
        return remote(block(q, h, y), block(q, h, y), down_s.at[q, s], down_r.at[q, s], below)

    def beside(q, h, k):
        side = lax.rem(y + k, ny)
        return remote(
            block(q, h, y), block(q, h, side), y_s.at[q, h, ny - 1 - k],
            y_r.at[q, h, ny - 1 - k], (g, z * ny + side),
        )

    def sideways(q, h, k):
        side = lax.rem(y + k, ny)
        return remote(
            block(q, h, y), block(q, h, y), y_s.at[q, h, k - 1], y_r.at[q, h, k - 1],
            (g, z * ny + side),
        )

    def share(q, h):
        for k in range(1, ny):
            sideways(q, h, k).start()

    def scatter(q):
        span = ny * slots
        for group in range(groups):
            stage[q, group * span : (group + 1) * span] = jnp.dot(
                place_ref[group * span : (group + 1) * span, :],
                rg_ref[:, cols(q, group)],
                preferred_element_type=jnp.float32,
            ).astype(jnp.bfloat16)

        def one(k, carry):
            plane(q, k).start()
            return carry

        lax.fori_loop(1, planes, one, 0)
        mine = pl.ds(pl.multiple_of(me * slots, slots), slots)
        recv[q, mine] = stage[q, mine]

    def gathered(q):
        def one(k, carry):
            plane(q, k).wait_recv()
            return carry

        lax.fori_loop(1, planes, one, 0)
        sums = jnp.dot(pick_ref[...], recv[q], preferred_element_type=jnp.float32)
        part[q] = sums
        to_line[q] = sums.astype(jnp.bfloat16)
        for k in range(1, nz):
            to_height(q, k).start()

    def total(q):
        here = line(z)
        acc = part[q, here]
        for k in range(1, nz):
            from_height(q, k).wait_recv()
            h = lax.rem(z + k, nz)
            acc = acc + from_line[q, line(h)].astype(jnp.float32)
        mine = pl.ds(pl.multiple_of((z * ny + y) * rows, rows), rows)
        piece[q, mine] = (og_ref[:, cols(q)].astype(jnp.float32) + acc).astype(jnp.bfloat16)

        @pl.when(z < nz - 1)
        def _():
            up(q, z, 0).start()

        @pl.when(z > 0)
        def _():
            down(q, z, 0).start()

        share(q, z)

    def forward(q, s):
        @pl.when(z - s >= 0)
        def _():
            up(q, z - s, s - 1).wait_recv()
            if s < nz - 1:
                @pl.when(z < nz - 1)
                def _():
                    up(q, z - s, s).start()
            share(q, z - s)

        @pl.when(z + s < nz)
        def _():
            down(q, z + s, s - 1).wait_recv()
            if s < nz - 1:
                @pl.when(z > 0)
                def _():
                    down(q, z + s, s).start()
            share(q, z + s)

    def project(q):
        for h in range(nz):
            for k in range(1, ny):
                beside(q, h, k).wait_recv()

        totals = piece[q]
        term = lax.dot_general(
            totals, wout_ref[:, cols(q)], (((1,), (1,)), ((), ())),
            preferred_element_type=jnp.float32,
        )

        @pl.when(q == 0)
        def _():
            ctx[...] = term

        @pl.when(q > 0)
        def _():
            ctx[...] += term

        share_of = lax.dot_general(
            context_ref[...], totals, (((1,), (0,)), ((), ())),
            preferred_element_type=jnp.float32,
        )

        @pl.when(q < parts - 1)
        def _():
            proj[q] = share_of.astype(jnp.bfloat16)
            to_owner(q).start()

        @pl.when(q == parts - 1)
        def _():
            acc = share_of
            for other in range(parts - 1):
                to_owner(other).wait_recv()
                acc = acc + proj_in[other].astype(jnp.float32)
            proj_ref[...] = acc.astype(jnp.bfloat16)
            ctx_ref[...] = ctx[...].astype(jnp.bfloat16)

    def to_owner(q):
        return remote(
            proj.at[q], proj_in.at[q], proj_s.at[q], proj_r.at[q],
            (owner(q, g), z * ny + y),
        )

    stages = [scatter, gathered, total]
    stages += [functools.partial(lambda s, q: forward(q, s), s) for s in range(1, nz)]
    stages += [project]

    last = len(stages) - 1

    def step(t, carry):
        for k in [*reversed(range(last)), last]:
            @pl.when((t >= k) & (t - k < parts))
            def _():
                stages[k](t - k)

        return carry

    lax.fori_loop(0, parts + last, step, 0)

    def drain(q, carry):
        def one(k, c):
            plane(q, k).wait_send()
            return c

        lax.fori_loop(1, planes, one, 0)
        for k in range(1, nz):
            to_height(q, k).wait_send()
        for h in range(nz):
            for k in range(1, ny):
                sideways(q, h, k).wait_send()
        for s in range(nz - 1):
            @pl.when((z - s >= 0) & (z < nz - 1))
            def _():
                up(q, z - s, s).wait_send()

            @pl.when((z + s < nz) & (z > 0))
            def _():
                down(q, z + s, s).wait_send()

        @pl.when(q < parts - 1)
        def _():
            to_owner(q).wait_send()

        return carry

    lax.fori_loop(0, parts, drain, 0)


def collect(row_grad, placer, picker, out_grad, context, w_out, groups, nz, ny):
    rows, width = out_grad.shape
    features = w_out.shape[0]
    taken = placer.shape[0]
    planes = groups * ny
    parts = groups
    chunk = width // parts
    tokens = nz * ny * rows
    dma = pltpu.SemaphoreType.DMA
    vmem = pl.BlockSpec(memory_space=pltpu.VMEM)
    line = (parts, nz * rows, chunk)
    return pl.pallas_call(
        collect_kernel,
        out_shape=(
            jax.ShapeDtypeStruct((tokens, features), jnp.bfloat16),
            jax.ShapeDtypeStruct((features, chunk), jnp.bfloat16),
        ),
        in_specs=[vmem] * 6,
        out_specs=(vmem, vmem),
        scratch_shapes=[
            pltpu.VMEM((parts, taken, chunk), jnp.bfloat16),
            pltpu.VMEM((parts, taken, chunk), jnp.bfloat16),
            pltpu.VMEM(line, jnp.float32),
            pltpu.VMEM((parts, tokens, chunk), jnp.bfloat16),
            pltpu.VMEM((tokens, features), jnp.float32),
            pltpu.VMEM((parts - 1, features, chunk), jnp.bfloat16),
            pltpu.VMEM((parts - 1, features, chunk), jnp.bfloat16),
            pltpu.VMEM(line, jnp.bfloat16),
            pltpu.VMEM(line, jnp.bfloat16),
            dma((parts, planes - 1)), dma((parts, planes - 1)),
            dma((parts, nz - 1)), dma((parts, nz - 1)),
            dma((parts, nz - 1)), dma((parts, nz - 1)),
            dma((parts, nz - 1)), dma((parts, nz - 1)),
            dma((parts, nz, ny - 1)), dma((parts, nz, ny - 1)),
            dma((parts - 1,)), dma((parts - 1,)),
        ],
        compiler_params=pltpu.CompilerParams(
            collective_id=1, has_side_effects=True, vmem_limit_bytes=40 * 2**20
        ),
    )(row_grad, placer, picker, out_grad, context, w_out)


def expert_backward(rows_in, rows_grad, scales, gate_w, up_w, down_w):
    gate_pre = jnp.dot(rows_in, gate_w, preferred_element_type=jnp.float32)
    up_pre = jnp.dot(rows_in, up_w, preferred_element_type=jnp.float32)
    sig = jax.nn.sigmoid(gate_pre)
    silu = gate_pre * sig
    hidden = (silu * up_pre).astype(jnp.bfloat16)
    scaled = (rows_grad.astype(jnp.float32) * scales[:, None]).astype(jnp.bfloat16)
    outer = (((0,), (0,)), ((), ()))
    inner_dims = (((1,), (1,)), ((), ()))
    back_hidden = lax.dot_general(scaled, down_w, inner_dims, preferred_element_type=jnp.float32)
    back_gate = (back_hidden * up_pre * sig * (1.0 + gate_pre * (1.0 - sig))).astype(jnp.bfloat16)
    back_up = (back_hidden * silu).astype(jnp.bfloat16)
    row_grad = lax.dot_general(back_gate, gate_w, inner_dims, preferred_element_type=jnp.float32)
    row_grad = row_grad + lax.dot_general(
        back_up, up_w, inner_dims, preferred_element_type=jnp.float32
    )
    grad_down = lax.dot_general(hidden, scaled, outer, preferred_element_type=jnp.float32).astype(
        jnp.bfloat16
    )
    grad_gate = lax.dot_general(
        rows_in, back_gate, outer, preferred_element_type=jnp.float32
    ).astype(jnp.bfloat16)
    grad_up = lax.dot_general(rows_in, back_up, outer, preferred_element_type=jnp.float32).astype(
        jnp.bfloat16
    )
    return (grad_gate, grad_up, grad_down, row_grad.astype(jnp.bfloat16))


def tables(selected, rows, most):
    groups, nz, ny, g, z, y = place()
    inner = nz * ny
    planes = groups * ny
    cap = selected.shape[1]
    me = g * ny + y
    experts = selected.reshape(groups, nz, ny, cap)
    experts = lax.dynamic_index_in_dim(experts, z, 1, keepdims=False).reshape(planes, cap)
    owner = experts // rows
    owner_z = (owner % inner) // ny
    owner_p = (owner // inner) * ny + owner % ny
    slot_range = jnp.arange(cap, dtype=jnp.int32)
    earlier = (owner[:, :, None] == owner[:, None, :]) & (
        slot_range[None, :, None] > slot_range[None, None, :]
    )
    ranking = jnp.sum(earlier.astype(jnp.int32), axis=2)
    slots = nz * most
    slot = owner_z * most + ranking
    token = owner_z * rows + experts % rows
    hit = (owner_p == me)[:, :, None] & (
        slot[:, :, None] == jnp.arange(slots, dtype=jnp.int32)[None, None, :]
    )
    table = jnp.sum(jnp.where(hit, token[:, :, None] + 1, 0), axis=1).reshape(-1)
    token_ids = jnp.arange(nz * rows, dtype=jnp.int32) + 1
    picker = (table[:, None] == token_ids[None, :]).astype(jnp.bfloat16)
    position = lax.dynamic_index_in_dim(owner_p * slots + slot, me, 0, keepdims=False)
    arrival = jnp.arange(planes * slots, dtype=jnp.int32)
    placer = (position[:, None] == arrival[None, :]).astype(jnp.bfloat16)
    return picker, placer


def body(moe_input, out_grad, context, gate_scale, selected, w_gate, w_up, w_down, w_out):
    groups = lax.axis_size("grp")
    inner_count = lax.axis_size("inner")
    devices = groups * inner_count
    nz, ny = split_inner(inner_count)
    planes = groups * ny
    tok_rows, width = moe_input.shape
    capacity = selected.shape[1]
    most = max(4, (2 * capacity + devices - 1) // devices)
    picker, placer = tables(selected, tok_rows, most)
    rows = dispatch(moe_input, out_grad, picker, placer, nz, planes)
    grad_gate, grad_up, grad_down, row_grad = expert_backward(
        rows[0], rows[1], gate_scale[0], w_gate[0], w_up[0], w_down[0]
    )
    grad_ctx, grad_proj = collect(
        row_grad, placer.T, picker.T, out_grad, context.T, w_out, groups, nz, ny
    )
    return (
        grad_gate[None],
        grad_up[None],
        grad_down[None],
        grad_ctx,
        grad_proj,
    )


def solution(mesh):
    placed = (
        P(("grp", "inner"), None),
        P(("grp", "inner"), None),
        P("grp", "inner"),
        P(("grp", "inner"), None),
        P(),
        P(("grp", "inner"), None, None),
        P(("grp", "inner"), None, None),
        P(("grp", "inner"), None, None),
        P("inner", None),
    )
    return jax.shard_map(
        body,
        mesh=mesh,
        in_specs=placed,
        out_specs=(
            P(("grp", "inner"), None, None),
            P(("grp", "inner"), None, None),
            P(("grp", "inner"), None, None),
            P("grp", "inner"),
            P("inner", "grp"),
        ),
        check_vma=False,
    )
```

```python
import functools

import jax
import jax.numpy as jnp
from jax import lax
from jax.experimental import pallas as pl
from jax.experimental.pallas import tpu as pltpu
from jax.sharding import PartitionSpec as P

MESH = pl.DeviceIdType.MESH


def split_inner(inner):
    across = 1
    while (2 * across) * (2 * across) <= inner:
        across *= 2
    return inner // across, across


def place():
    groups = lax.axis_size("grp")
    inner = lax.axis_size("inner")
    nz, ny = split_inner(inner)
    g = lax.axis_index("grp")
    i = lax.axis_index("inner")
    z = i // ny
    y = i % ny
    return groups, nz, ny, g, z, y


def at_plane(k, z, ny):
    return (k // ny, z * ny + k % ny)


def greet(g, z, y, nz, ny, planes):
    me = g * ny + y
    barrier = pltpu.get_barrier_semaphore()

    for k in range(1, nz):
        height = lax.rem(z + k, nz)
        pl.semaphore_signal(barrier, inc=1, device_id=(g, height * ny + y), device_id_type=MESH)

    def one(k, carry):
        peer = lax.rem(me + k, planes)
        pl.semaphore_signal(barrier, inc=1, device_id=at_plane(peer, z, ny), device_id_type=MESH)
        return carry

    lax.fori_loop(1, planes, one, 0)
    pl.semaphore_wait(barrier, planes - 1 + nz - 1)


def remote(src, dst, send, recv, device):
    return pltpu.make_async_remote_copy(
        src_ref=src, dst_ref=dst, send_sem=send, recv_sem=recv, device_id=device, device_id_type=MESH
    )


def dispatch_kernel(
    chunk, in_ref, grad_ref, gate_hbm, up_hbm, down_hbm, pick_ref, place_ref, scale_ref,
    rows_ref, scaled_ref, gate_ref, upper_ref, back_ref, gat, stage, recv, gate_w, up_w, down_w,
    up_s, up_r, down_s, down_r, plane_s, plane_r, own_s, w_s,
):
    groups, nz, ny, g, z, y = place()
    planes = groups * ny
    me = g * ny + y
    rows, width = in_ref.shape
    slots = stage.shape[1] // planes
    parts = width // chunk
    items = 2 * parts
    ahead = 3
    above = (g, (z + 1) * ny + y)
    below = (g, (z - 1) * ny + y)
    here = pl.ds(pl.multiple_of(z * rows, rows), rows)

    def fetch(i):
        ref = in_ref if i < parts else grad_ref
        taken = ref.at[:, pl.ds((i % parts) * chunk, chunk)]
        return pltpu.make_async_copy(taken, gat.at[i, here], own_s.at[i])

    weights = [
        pltpu.make_async_copy(src, dst, w_s.at[n])
        for n, (src, dst) in enumerate([(gate_hbm, gate_w), (up_hbm, up_w), (down_hbm, down_w)])
    ]
    for i in range(items):
        fetch(i).start()
    for copy in weights:
        copy.start()
    greet(g, z, y, nz, ny, planes)

    def cols(i):
        return pl.ds(pl.multiple_of((i % parts) * chunk, chunk), chunk)

    def block(i, h):
        return gat.at[i, pl.ds(pl.multiple_of(h * rows, rows), rows)]

    def up(i, h, s):
        return remote(block(i, h), block(i, h), up_s.at[i, s], up_r.at[i, s], above)

    def down(i, h, s):
        return remote(block(i, h), block(i, h), down_s.at[i, s], down_r.at[i, s], below)

    def own(i):
        @pl.when(z < nz - 1)
        def _():
            up(i, z, 0).start()

        @pl.when(z > 0)
        def _():
            down(i, z, 0).start()

    def hops(i):
        for s in range(1, nz):
            @pl.when(z - s >= 0)
            def _():
                up(i, z - s, s - 1).wait_recv()

            if s < nz - 1:
                @pl.when((z - s >= 0) & (z < nz - 1))
                def _():
                    up(i, z - s, s).start()

            @pl.when(z + s < nz)
            def _():
                down(i, z + s, s - 1).wait_recv()

            if s < nz - 1:
                @pl.when((z + s < nz) & (z > 0))
                def _():
                    down(i, z + s, s).start()

    def plane(i, k):
        peer = lax.rem(me + k, planes)
        theirs = pl.ds(pl.multiple_of(peer * slots, slots), slots)
        mine = pl.ds(pl.multiple_of(me * slots, slots), slots)
        return remote(
            stage.at[i, theirs], recv.at[i, mine],
            plane_s.at[i, k - 1], plane_r.at[i, k - 1], at_plane(peer, z, ny),
        )

    def pick(i):
        stage[i] = jnp.dot(
            pick_ref[...], gat[i], preferred_element_type=jnp.float32
        ).astype(jnp.bfloat16)

        def one(k, carry):
            plane(i, k).start()
            return carry

        lax.fori_loop(1, planes, one, 0)
        mine = pl.ds(pl.multiple_of(me * slots, slots), slots)
        recv[i, mine] = stage[i, mine]

    def finish(i):
        a = i // parts

        def one(k, carry):
            plane(i, k).wait_recv()
            return carry

        lax.fori_loop(1, planes, one, 0)
        rows = jnp.dot(
            place_ref[...], recv[i], preferred_element_type=jnp.float32
        ).astype(jnp.bfloat16)

        @pl.when(i == 0)
        def _():
            weights[0].wait()
            weights[1].wait()
            weights[2].wait()

        @pl.when(a == 0)
        def _():
            rows_ref[:, cols(i)] = rows
            gate_ref[...] += jnp.dot(rows, gate_w[cols(i), :], preferred_element_type=jnp.float32)
            upper_ref[...] += jnp.dot(rows, up_w[cols(i), :], preferred_element_type=jnp.float32)

        @pl.when(a == 1)
        def _():
            scaled = (rows.astype(jnp.float32) * scale_ref[...]).astype(jnp.bfloat16)
            scaled_ref[:, cols(i)] = scaled
            back_ref[...] += lax.dot_general(
                scaled, down_w[:, cols(i)], (((1,), (1,)), ((), ())),
                preferred_element_type=jnp.float32,
            )

    gate_ref[...] = jnp.zeros_like(gate_ref)
    upper_ref[...] = jnp.zeros_like(upper_ref)
    back_ref[...] = jnp.zeros_like(back_ref)
    for i in range(items):
        fetch(i).wait()

    for i in range(ahead):
        own(i)

    def step(i, carry):
        @pl.when(i + ahead < items)
        def _():
            own(i + ahead)

        hops(i)
        pick(i)

        @pl.when(i > 1)
        def _():
            finish(i - 2)

        return carry

    lax.fori_loop(0, items, step, 0)
    finish(items - 2)
    finish(items - 1)

    def drain(i, carry):
        for s in range(nz - 1):
            @pl.when((z - s >= 0) & (z < nz - 1))
            def _():
                up(i, z - s, s).wait_send()

            @pl.when((z + s < nz) & (z > 0))
            def _():
                down(i, z + s, s).wait_send()

        def one(k, c):
            plane(i, k).wait_send()
            return c

        return lax.fori_loop(1, planes, one, carry)

    lax.fori_loop(0, items, drain, 0)


def dispatch(moe_input, out_grad, gate_w, up_w, down_w, picker, placer, scales, nz, planes):
    rows, width = moe_input.shape
    hidden = gate_w.shape[1]
    taken = placer.shape[1]
    cap = placer.shape[0]
    chunk = width // 4
    items = 2 * (width // chunk)
    dma = pltpu.SemaphoreType.DMA
    vmem = pl.BlockSpec(memory_space=pltpu.VMEM)
    return pl.pallas_call(
        functools.partial(dispatch_kernel, chunk),
        out_shape=[jax.ShapeDtypeStruct((cap, width), jnp.bfloat16)] * 2
        + [jax.ShapeDtypeStruct((cap, hidden), jnp.float32)] * 3,
        in_specs=[pl.BlockSpec(memory_space=pl.ANY)] * 5 + [vmem] * 3,
        out_specs=[vmem] * 5,
        scratch_shapes=[
            pltpu.VMEM((items, nz * rows, chunk), jnp.bfloat16),
            pltpu.VMEM((items, taken, chunk), jnp.bfloat16),
            pltpu.VMEM((items, taken, chunk), jnp.bfloat16),
            pltpu.VMEM(gate_w.shape, jnp.bfloat16),
            pltpu.VMEM(up_w.shape, jnp.bfloat16),
            pltpu.VMEM(down_w.shape, jnp.bfloat16),
            dma((items, nz - 1)), dma((items, nz - 1)),
            dma((items, nz - 1)), dma((items, nz - 1)),
            dma((items, planes - 1)), dma((items, planes - 1)),
            dma((items,)), dma((3,)),
        ],
        compiler_params=pltpu.CompilerParams(
            collective_id=0, has_side_effects=True, vmem_limit_bytes=48 * 2**20
        ),
    )(moe_input, out_grad, gate_w, up_w, down_w, picker, placer, scales)


def collect_kernel(
    rg_ref, place_ref, pick_ref, og_ref, context_ref, wout_ref, ctx_ref, proj_ref,
    stage, recv, part, piece, ctx, proj, proj_in, to_line, from_line, context_t,
    plane_s, plane_r, sum_s, sum_r, up_s, up_r, down_s, down_r, y_s, y_r, proj_s, proj_r,
):
    groups, nz, ny, g, z, y = place()
    planes = groups * ny
    me = g * ny + y
    rows, width = og_ref.shape
    slots = stage.shape[1] // planes
    parts = groups
    chunk = width // parts
    above = (g, (z + 1) * ny + y)
    below = (g, (z - 1) * ny + y)
    greet(g, z, y, nz, ny, planes)

    def owner(q, group):
        return lax.rem(group + q + 1, groups)

    def cols(q, group=g):
        return pl.ds(pl.multiple_of(owner(q, group) * chunk, chunk), chunk)

    def line(h):
        return pl.ds(pl.multiple_of(h * rows, rows), rows)

    def plane(q, k):
        peer = lax.rem(me + k, planes)
        theirs = pl.ds(pl.multiple_of(peer * slots, slots), slots)
        mine = pl.ds(pl.multiple_of(me * slots, slots), slots)
        return remote(
            stage.at[q, theirs], recv.at[q, mine],
            plane_s.at[q, k - 1], plane_r.at[q, k - 1], at_plane(peer, z, ny),
        )

    def to_height(q, k):
        h = lax.rem(z + k, nz)
        return remote(
            to_line.at[q, line(h)], from_line.at[q, line(z)],
            sum_s.at[q, k - 1], sum_r.at[q, k - 1], (g, h * ny + y),
        )

    def from_height(q, k):
        h = lax.rem(z + k, nz)
        return remote(
            to_line.at[q, line(h)], from_line.at[q, line(h)],
            sum_s.at[q, nz - 1 - k], sum_r.at[q, nz - 1 - k], (g, h * ny + y),
        )

    def block(q, h, side):
        return piece.at[q, pl.ds(pl.multiple_of((h * ny + side) * rows, rows), rows)]

    def up(q, h, s):
        return remote(block(q, h, y), block(q, h, y), up_s.at[q, s], up_r.at[q, s], above)

    def down(q, h, s):
        return remote(block(q, h, y), block(q, h, y), down_s.at[q, s], down_r.at[q, s], below)

    def beside(q, h, k):
        side = lax.rem(y + k, ny)
        return remote(
            block(q, h, y), block(q, h, side), y_s.at[q, h, ny - 1 - k],
            y_r.at[q, h, ny - 1 - k], (g, z * ny + side),
        )

    def sideways(q, h, k):
        side = lax.rem(y + k, ny)
        return remote(
            block(q, h, y), block(q, h, y), y_s.at[q, h, k - 1], y_r.at[q, h, k - 1],
            (g, z * ny + side),
        )

    def share(q, h):
        for k in range(1, ny):
            sideways(q, h, k).start()

    def scatter(q):
        span = ny * slots
        for group in range(groups):
            stage[q, group * span : (group + 1) * span] = jnp.dot(
                place_ref[group * span : (group + 1) * span, :],
                rg_ref[:, cols(q, group)],
                preferred_element_type=jnp.float32,
            ).astype(jnp.bfloat16)

        def one(k, carry):
            plane(q, k).start()
            return carry

        lax.fori_loop(1, planes, one, 0)
        mine = pl.ds(pl.multiple_of(me * slots, slots), slots)
        recv[q, mine] = stage[q, mine]

    def gathered(q):
        def one(k, carry):
            plane(q, k).wait_recv()
            return carry

        lax.fori_loop(1, planes, one, 0)
        sums = jnp.dot(pick_ref[...], recv[q], preferred_element_type=jnp.float32)
        part[q] = sums
        to_line[q] = sums.astype(jnp.bfloat16)
        for k in range(1, nz):
            to_height(q, k).start()

    def total(q):
        here = line(z)
        acc = part[q, here]
        for k in range(1, nz):
            from_height(q, k).wait_recv()
            h = lax.rem(z + k, nz)
            acc = acc + from_line[q, line(h)].astype(jnp.float32)
        mine = pl.ds(pl.multiple_of((z * ny + y) * rows, rows), rows)
        piece[q, mine] = (og_ref[:, cols(q)].astype(jnp.float32) + acc).astype(jnp.bfloat16)

        @pl.when(z < nz - 1)
        def _():
            up(q, z, 0).start()

        @pl.when(z > 0)
        def _():
            down(q, z, 0).start()

        share(q, z)

    def forward(q, s):
        @pl.when(z - s >= 0)
        def _():
            up(q, z - s, s - 1).wait_recv()
            if s < nz - 1:
                @pl.when(z < nz - 1)
                def _():
                    up(q, z - s, s).start()
            share(q, z - s)

        @pl.when(z + s < nz)
        def _():
            down(q, z + s, s - 1).wait_recv()
            if s < nz - 1:
                @pl.when(z > 0)
                def _():
                    down(q, z + s, s).start()
            share(q, z + s)

    def project(q):
        for h in range(nz):
            for k in range(1, ny):
                beside(q, h, k).wait_recv()

        totals = piece[q]
        term = lax.dot_general(
            totals, wout_ref[:, cols(q)], (((1,), (1,)), ((), ())),
            preferred_element_type=jnp.float32,
        )

        @pl.when(q == 0)
        def _():
            ctx[...] = term

        @pl.when(q > 0)
        def _():
            ctx[...] += term

        share_of = lax.dot_general(
            context_t[...], totals, (((1,), (0,)), ((), ())),
            preferred_element_type=jnp.float32,
        )

        @pl.when(q < parts - 1)
        def _():
            proj[q] = share_of.astype(jnp.bfloat16)
            to_owner(q).start()

        @pl.when(q == parts - 1)
        def _():
            acc = share_of
            for other in range(parts - 1):
                to_owner(other).wait_recv()
                acc = acc + proj_in[other].astype(jnp.float32)
            proj_ref[...] = acc.astype(jnp.bfloat16)
            ctx_ref[...] = ctx[...].astype(jnp.bfloat16)

    def to_owner(q):
        return remote(
            proj.at[q], proj_in.at[q], proj_s.at[q], proj_r.at[q],
            (owner(q, g), z * ny + y),
        )

    stages = [scatter, gathered, total]
    stages += [functools.partial(lambda s, q: forward(q, s), s) for s in range(1, nz)]
    stages += [project]

    last = len(stages) - 1

    def step(t, carry):
        for k in [*reversed(range(last)), last]:
            @pl.when((t >= k) & (t - k < parts))
            def _():
                stages[k](t - k)

        @pl.when(t == 0)
        def _():
            context_t[...] = context_ref[...].T

        return carry

    lax.fori_loop(0, parts + last, step, 0)

    def drain(q, carry):
        def one(k, c):
            plane(q, k).wait_send()
            return c

        lax.fori_loop(1, planes, one, 0)
        for k in range(1, nz):
            to_height(q, k).wait_send()
        for h in range(nz):
            for k in range(1, ny):
                sideways(q, h, k).wait_send()
        for s in range(nz - 1):
            @pl.when((z - s >= 0) & (z < nz - 1))
            def _():
                up(q, z - s, s).wait_send()

            @pl.when((z + s < nz) & (z > 0))
            def _():
                down(q, z + s, s).wait_send()

        @pl.when(q < parts - 1)
        def _():
            to_owner(q).wait_send()

        return carry

    lax.fori_loop(0, parts, drain, 0)


def collect(row_grad, placer, picker, out_grad, context, w_out, groups, nz, ny):
    rows, width = out_grad.shape
    features = w_out.shape[0]
    taken = placer.shape[0]
    planes = groups * ny
    parts = groups
    chunk = width // parts
    tokens = nz * ny * rows
    dma = pltpu.SemaphoreType.DMA
    vmem = pl.BlockSpec(memory_space=pltpu.VMEM)
    line = (parts, nz * rows, chunk)
    return pl.pallas_call(
        collect_kernel,
        out_shape=(
            jax.ShapeDtypeStruct((tokens, features), jnp.bfloat16),
            jax.ShapeDtypeStruct((features, chunk), jnp.bfloat16),
        ),
        in_specs=[vmem] * 6,
        out_specs=(vmem, vmem),
        scratch_shapes=[
            pltpu.VMEM((parts, taken, chunk), jnp.bfloat16),
            pltpu.VMEM((parts, taken, chunk), jnp.bfloat16),
            pltpu.VMEM(line, jnp.float32),
            pltpu.VMEM((parts, tokens, chunk), jnp.bfloat16),
            pltpu.VMEM((tokens, features), jnp.float32),
            pltpu.VMEM((parts - 1, features, chunk), jnp.bfloat16),
            pltpu.VMEM((parts - 1, features, chunk), jnp.bfloat16),
            pltpu.VMEM(line, jnp.bfloat16),
            pltpu.VMEM(line, jnp.bfloat16),
            pltpu.VMEM((features, tokens), jnp.bfloat16),
            dma((parts, planes - 1)), dma((parts, planes - 1)),
            dma((parts, nz - 1)), dma((parts, nz - 1)),
            dma((parts, nz - 1)), dma((parts, nz - 1)),
            dma((parts, nz - 1)), dma((parts, nz - 1)),
            dma((parts, nz, ny - 1)), dma((parts, nz, ny - 1)),
            dma((parts - 1,)), dma((parts - 1,)),
        ],
        compiler_params=pltpu.CompilerParams(
            collective_id=1, has_side_effects=True, vmem_limit_bytes=44 * 2**20
        ),
    )(row_grad, placer, picker, out_grad, context, w_out)


def expert_backward(rows_in, scaled, gate_pre, up_pre, back_hidden, gate_w, up_w):
    sig = jax.nn.sigmoid(gate_pre)
    silu = gate_pre * sig
    hidden = (silu * up_pre).astype(jnp.bfloat16)
    outer = (((0,), (0,)), ((), ()))
    inner_dims = (((1,), (1,)), ((), ()))
    back_gate = (back_hidden * up_pre * sig * (1.0 + gate_pre * (1.0 - sig))).astype(jnp.bfloat16)
    back_up = (back_hidden * silu).astype(jnp.bfloat16)
    row_grad = lax.dot_general(back_gate, gate_w, inner_dims, preferred_element_type=jnp.float32)
    row_grad = row_grad + lax.dot_general(
        back_up, up_w, inner_dims, preferred_element_type=jnp.float32
    )
    grad_down = lax.dot_general(hidden, scaled, outer, preferred_element_type=jnp.float32).astype(
        jnp.bfloat16
    )
    grad_gate = lax.dot_general(
        rows_in, back_gate, outer, preferred_element_type=jnp.float32
    ).astype(jnp.bfloat16)
    grad_up = lax.dot_general(rows_in, back_up, outer, preferred_element_type=jnp.float32).astype(
        jnp.bfloat16
    )
    return (grad_gate, grad_up, grad_down, row_grad.astype(jnp.bfloat16))


def tables(selected, rows, most):
    groups, nz, ny, g, z, y = place()
    inner = nz * ny
    planes = groups * ny
    cap = selected.shape[1]
    me = g * ny + y
    experts = selected.reshape(groups, nz, ny, cap)
    experts = lax.dynamic_index_in_dim(experts, z, 1, keepdims=False).reshape(planes, cap)
    owner = experts // rows
    owner_z = (owner % inner) // ny
    owner_p = (owner // inner) * ny + owner % ny
    slot_range = jnp.arange(cap, dtype=jnp.int32)
    earlier = (owner[:, :, None] == owner[:, None, :]) & (
        slot_range[None, :, None] > slot_range[None, None, :]
    )
    ranking = jnp.sum(earlier.astype(jnp.int32), axis=2)
    slots = nz * most
    slot = owner_z * most + ranking
    token = owner_z * rows + experts % rows
    hit = (owner_p == me)[:, :, None] & (
        slot[:, :, None] == jnp.arange(slots, dtype=jnp.int32)[None, None, :]
    )
    table = jnp.sum(jnp.where(hit, token[:, :, None] + 1, 0), axis=1).reshape(-1)
    token_ids = jnp.arange(nz * rows, dtype=jnp.int32) + 1
    picker = (table[:, None] == token_ids[None, :]).astype(jnp.bfloat16)
    position = lax.dynamic_index_in_dim(owner_p * slots + slot, me, 0, keepdims=False)
    arrival = jnp.arange(planes * slots, dtype=jnp.int32)
    placer = (position[:, None] == arrival[None, :]).astype(jnp.bfloat16)
    return picker, placer


def body(moe_input, out_grad, context, gate_scale, selected, w_gate, w_up, w_down, w_out):
    groups = lax.axis_size("grp")
    inner_count = lax.axis_size("inner")
    devices = groups * inner_count
    nz, ny = split_inner(inner_count)
    planes = groups * ny
    tok_rows, width = moe_input.shape
    capacity = selected.shape[1]
    most = max(4, (2 * capacity + devices - 1) // devices)
    picker, placer = tables(selected, tok_rows, most)
    rows_in, scaled, gate_pre, up_pre, back_hidden = dispatch(
        moe_input, out_grad, w_gate[0], w_up[0], w_down[0], picker, placer,
        gate_scale[0][:, None], nz, planes,
    )
    grad_gate, grad_up, grad_down, row_grad = expert_backward(
        rows_in, scaled, gate_pre, up_pre, back_hidden, w_gate[0], w_up[0]
    )
    grad_ctx, grad_proj = collect(
        row_grad, placer.T, picker.T, out_grad, context, w_out, groups, nz, ny
    )
    return (
        grad_gate[None],
        grad_up[None],
        grad_down[None],
        grad_ctx,
        grad_proj,
    )


def solution(mesh):
    placed = (
        P(("grp", "inner"), None),
        P(("grp", "inner"), None),
        P("grp", "inner"),
        P(("grp", "inner"), None),
        P(),
        P(("grp", "inner"), None, None),
        P(("grp", "inner"), None, None),
        P(("grp", "inner"), None, None),
        P("inner", None),
    )
    return jax.shard_map(
        body,
        mesh=mesh,
        in_specs=placed,
        out_specs=(
            P(("grp", "inner"), None, None),
            P(("grp", "inner"), None, None),
            P(("grp", "inner"), None, None),
            P("grp", "inner"),
            P("inner", "grp"),
        ),
        check_vma=False,
    )
```

```python
import functools

import jax
import jax.numpy as jnp
from jax import lax
from jax.experimental import pallas as pl
from jax.experimental.pallas import tpu as pltpu
from jax.sharding import PartitionSpec as P

MESH = pl.DeviceIdType.MESH


def split_inner(inner):
    across = 1
    while (2 * across) * (2 * across) <= inner:
        across *= 2
    return inner // across, across


def place():
    groups = lax.axis_size("grp")
    inner = lax.axis_size("inner")
    nz, ny = split_inner(inner)
    g = lax.axis_index("grp")
    i = lax.axis_index("inner")
    z = i // ny
    y = i % ny
    return groups, nz, ny, g, z, y


def at_plane(k, z, ny):
    return (k // ny, z * ny + k % ny)


def greet(g, z, y, nz, ny, planes):
    me = g * ny + y
    barrier = pltpu.get_barrier_semaphore()

    for k in range(1, nz):
        height = lax.rem(z + k, nz)
        pl.semaphore_signal(barrier, inc=1, device_id=(g, height * ny + y), device_id_type=MESH)

    def one(k, carry):
        peer = lax.rem(me + k, planes)
        pl.semaphore_signal(barrier, inc=1, device_id=at_plane(peer, z, ny), device_id_type=MESH)
        return carry

    lax.fori_loop(1, planes, one, 0)
    pl.semaphore_wait(barrier, planes - 1 + nz - 1)


def remote(src, dst, send, recv, device):
    return pltpu.make_async_remote_copy(
        src_ref=src, dst_ref=dst, send_sem=send, recv_sem=recv, device_id=device, device_id_type=MESH
    )


def dispatch_kernel(
    chunk, in_ref, grad_ref, gate_hbm, up_hbm, down_hbm, pick_ref, place_ref, scale_ref,
    rows_ref, scaled_ref, gate_ref, upper_ref, back_ref, gat, stage, recv, gate_w, up_w, down_w,
    up_s, up_r, down_s, down_r, plane_s, plane_r, own_s, w_s,
):
    groups, nz, ny, g, z, y = place()
    planes = groups * ny
    me = g * ny + y
    rows, width = in_ref.shape
    slots = stage.shape[1] // planes
    parts = width // chunk
    items = 2 * parts
    ahead = 3
    above = (g, (z + 1) * ny + y)
    below = (g, (z - 1) * ny + y)
    here = pl.ds(pl.multiple_of(z * rows, rows), rows)

    def fetch(i):
        ref = in_ref if i < parts else grad_ref
        taken = ref.at[:, pl.ds((i % parts) * chunk, chunk)]
        return pltpu.make_async_copy(taken, gat.at[i, here], own_s.at[i])

    weights = [
        pltpu.make_async_copy(src, dst, w_s.at[n])
        for n, (src, dst) in enumerate([(gate_hbm, gate_w), (up_hbm, up_w), (down_hbm, down_w)])
    ]
    for i in range(items):
        fetch(i).start()
    for copy in weights:
        copy.start()
    greet(g, z, y, nz, ny, planes)

    def cols(i):
        return pl.ds(pl.multiple_of((i % parts) * chunk, chunk), chunk)

    def block(i, h):
        return gat.at[i, pl.ds(pl.multiple_of(h * rows, rows), rows)]

    def up(i, h, s):
        return remote(block(i, h), block(i, h), up_s.at[i, s], up_r.at[i, s], above)

    def down(i, h, s):
        return remote(block(i, h), block(i, h), down_s.at[i, s], down_r.at[i, s], below)

    def own(i):
        @pl.when(z < nz - 1)
        def _():
            up(i, z, 0).start()

        @pl.when(z > 0)
        def _():
            down(i, z, 0).start()

    def hops(i):
        for s in range(1, nz):
            @pl.when(z - s >= 0)
            def _():
                up(i, z - s, s - 1).wait_recv()

            if s < nz - 1:
                @pl.when((z - s >= 0) & (z < nz - 1))
                def _():
                    up(i, z - s, s).start()

            @pl.when(z + s < nz)
            def _():
                down(i, z + s, s - 1).wait_recv()

            if s < nz - 1:
                @pl.when((z + s < nz) & (z > 0))
                def _():
                    down(i, z + s, s).start()

    def plane(i, k):
        peer = lax.rem(me + k, planes)
        theirs = pl.ds(pl.multiple_of(peer * slots, slots), slots)
        mine = pl.ds(pl.multiple_of(me * slots, slots), slots)
        return remote(
            stage.at[i, theirs], recv.at[i, mine],
            plane_s.at[i, k - 1], plane_r.at[i, k - 1], at_plane(peer, z, ny),
        )

    def pick(i):
        stage[i] = jnp.dot(
            pick_ref[...], gat[i], preferred_element_type=jnp.float32
        ).astype(jnp.bfloat16)

        def one(k, carry):
            plane(i, k).start()
            return carry

        lax.fori_loop(1, planes, one, 0)
        mine = pl.ds(pl.multiple_of(me * slots, slots), slots)
        recv[i, mine] = stage[i, mine]

    def finish(i):
        a = i // parts

        def one(k, carry):
            plane(i, k).wait_recv()
            return carry

        lax.fori_loop(1, planes, one, 0)
        rows = jnp.dot(
            place_ref[...], recv[i], preferred_element_type=jnp.float32
        ).astype(jnp.bfloat16)

        @pl.when(i == 0)
        def _():
            weights[0].wait()
            weights[1].wait()
            weights[2].wait()

        @pl.when(a == 0)
        def _():
            rows_ref[:, cols(i)] = rows
            gate_ref[...] += jnp.dot(rows, gate_w[cols(i), :], preferred_element_type=jnp.float32)
            upper_ref[...] += jnp.dot(rows, up_w[cols(i), :], preferred_element_type=jnp.float32)

        @pl.when(a == 1)
        def _():
            scaled = (rows.astype(jnp.float32) * scale_ref[...]).astype(jnp.bfloat16)
            scaled_ref[:, cols(i)] = scaled
            back_ref[...] += lax.dot_general(
                scaled, down_w[:, cols(i)], (((1,), (1,)), ((), ())),
                preferred_element_type=jnp.float32,
            )

    gate_ref[...] = jnp.zeros_like(gate_ref)
    upper_ref[...] = jnp.zeros_like(upper_ref)
    back_ref[...] = jnp.zeros_like(back_ref)
    for i in range(items):
        fetch(i).wait()

    for i in range(ahead):
        own(i)

    def step(i, carry):
        @pl.when(i + ahead < items)
        def _():
            own(i + ahead)

        hops(i)
        pick(i)

        @pl.when(i > 1)
        def _():
            finish(i - 2)

        return carry

    lax.fori_loop(0, items, step, 0)
    finish(items - 2)
    finish(items - 1)

    def drain(i, carry):
        for s in range(nz - 1):
            @pl.when((z - s >= 0) & (z < nz - 1))
            def _():
                up(i, z - s, s).wait_send()

            @pl.when((z + s < nz) & (z > 0))
            def _():
                down(i, z + s, s).wait_send()

        def one(k, c):
            plane(i, k).wait_send()
            return c

        return lax.fori_loop(1, planes, one, carry)

    lax.fori_loop(0, items, drain, 0)


def dispatch(moe_input, out_grad, gate_w, up_w, down_w, picker, placer, scales, nz, planes):
    rows, width = moe_input.shape
    hidden = gate_w.shape[1]
    taken = placer.shape[1]
    cap = placer.shape[0]
    chunk = width // 4
    items = 2 * (width // chunk)
    dma = pltpu.SemaphoreType.DMA
    vmem = pl.BlockSpec(memory_space=pltpu.VMEM)
    return pl.pallas_call(
        functools.partial(dispatch_kernel, chunk),
        out_shape=[jax.ShapeDtypeStruct((cap, width), jnp.bfloat16)] * 2
        + [jax.ShapeDtypeStruct((cap, hidden), jnp.float32)] * 3,
        in_specs=[pl.BlockSpec(memory_space=pl.ANY)] * 5 + [vmem] * 3,
        out_specs=[vmem] * 5,
        scratch_shapes=[
            pltpu.VMEM((items, nz * rows, chunk), jnp.bfloat16),
            pltpu.VMEM((items, taken, chunk), jnp.bfloat16),
            pltpu.VMEM((items, taken, chunk), jnp.bfloat16),
            pltpu.VMEM(gate_w.shape, jnp.bfloat16),
            pltpu.VMEM(up_w.shape, jnp.bfloat16),
            pltpu.VMEM(down_w.shape, jnp.bfloat16),
            dma((items, nz - 1)), dma((items, nz - 1)),
            dma((items, nz - 1)), dma((items, nz - 1)),
            dma((items, planes - 1)), dma((items, planes - 1)),
            dma((items,)), dma((3,)),
        ],
        compiler_params=pltpu.CompilerParams(
            collective_id=0, has_side_effects=True, vmem_limit_bytes=58 * 2**20
        ),
    )(moe_input, out_grad, gate_w, up_w, down_w, picker, placer, scales)


def collect_kernel(
    rg_ref, place_ref, pick_ref, og_ref, context_ref, wout_ref, ctx_ref, proj_ref,
    stage, recv, part, piece, ctx, proj, proj_in, to_line, from_line, context_t,
    plane_s, plane_r, sum_s, sum_r, up_s, up_r, down_s, down_r, y_s, y_r, proj_s, proj_r,
):
    groups, nz, ny, g, z, y = place()
    planes = groups * ny
    me = g * ny + y
    rows, width = og_ref.shape
    slots = stage.shape[1] // planes
    parts = groups
    chunk = width // parts
    above = (g, (z + 1) * ny + y)
    below = (g, (z - 1) * ny + y)
    greet(g, z, y, nz, ny, planes)

    def owner(q, group):
        return lax.rem(group + q + 1, groups)

    def cols(q, group=g):
        return pl.ds(pl.multiple_of(owner(q, group) * chunk, chunk), chunk)

    def line(h):
        return pl.ds(pl.multiple_of(h * rows, rows), rows)

    def plane(q, k):
        peer = lax.rem(me + k, planes)
        theirs = pl.ds(pl.multiple_of(peer * slots, slots), slots)
        mine = pl.ds(pl.multiple_of(me * slots, slots), slots)
        return remote(
            stage.at[q, theirs], recv.at[q, mine],
            plane_s.at[q, k - 1], plane_r.at[q, k - 1], at_plane(peer, z, ny),
        )

    def to_height(q, k):
        h = lax.rem(z + k, nz)
        return remote(
            to_line.at[q, line(h)], from_line.at[q, line(z)],
            sum_s.at[q, k - 1], sum_r.at[q, k - 1], (g, h * ny + y),
        )

    def from_height(q, k):
        h = lax.rem(z + k, nz)
        return remote(
            to_line.at[q, line(h)], from_line.at[q, line(h)],
            sum_s.at[q, nz - 1 - k], sum_r.at[q, nz - 1 - k], (g, h * ny + y),
        )

    def block(q, h, side):
        return piece.at[q, pl.ds(pl.multiple_of((h * ny + side) * rows, rows), rows)]

    def up(q, h, s):
        return remote(block(q, h, y), block(q, h, y), up_s.at[q, s], up_r.at[q, s], above)

    def down(q, h, s):
        return remote(block(q, h, y), block(q, h, y), down_s.at[q, s], down_r.at[q, s], below)

    def beside(q, h, k):
        side = lax.rem(y + k, ny)
        return remote(
            block(q, h, y), block(q, h, side), y_s.at[q, h, ny - 1 - k],
            y_r.at[q, h, ny - 1 - k], (g, z * ny + side),
        )

    def sideways(q, h, k):
        side = lax.rem(y + k, ny)
        return remote(
            block(q, h, y), block(q, h, y), y_s.at[q, h, k - 1], y_r.at[q, h, k - 1],
            (g, z * ny + side),
        )

    def share(q, h):
        for k in range(1, ny):
            sideways(q, h, k).start()

    def scatter(q):
        span = ny * slots
        for group in range(groups):
            stage[q, group * span : (group + 1) * span] = jnp.dot(
                place_ref[group * span : (group + 1) * span, :],
                rg_ref[:, cols(q, group)],
                preferred_element_type=jnp.float32,
            ).astype(jnp.bfloat16)

        def one(k, carry):
            plane(q, k).start()
            return carry

        lax.fori_loop(1, planes, one, 0)
        mine = pl.ds(pl.multiple_of(me * slots, slots), slots)
        recv[q, mine] = stage[q, mine]

    def gathered(q):
        def one(k, carry):
            plane(q, k).wait_recv()
            return carry

        lax.fori_loop(1, planes, one, 0)
        sums = jnp.dot(pick_ref[...], recv[q], preferred_element_type=jnp.float32)
        part[q] = sums
        to_line[q] = sums.astype(jnp.bfloat16)
        for k in range(1, nz):
            to_height(q, k).start()

    def total(q):
        here = line(z)
        acc = part[q, here]
        for k in range(1, nz):
            from_height(q, k).wait_recv()
            h = lax.rem(z + k, nz)
            acc = acc + from_line[q, line(h)].astype(jnp.float32)
        mine = pl.ds(pl.multiple_of((z * ny + y) * rows, rows), rows)
        piece[q, mine] = (og_ref[:, cols(q)].astype(jnp.float32) + acc).astype(jnp.bfloat16)

        @pl.when(z < nz - 1)
        def _():
            up(q, z, 0).start()

        @pl.when(z > 0)
        def _():
            down(q, z, 0).start()

        share(q, z)

    def forward(q, s):
        @pl.when(z - s >= 0)
        def _():
            up(q, z - s, s - 1).wait_recv()
            if s < nz - 1:
                @pl.when(z < nz - 1)
                def _():
                    up(q, z - s, s).start()
            share(q, z - s)

        @pl.when(z + s < nz)
        def _():
            down(q, z + s, s - 1).wait_recv()
            if s < nz - 1:
                @pl.when(z > 0)
                def _():
                    down(q, z + s, s).start()
            share(q, z + s)

    def project(q):
        for h in range(nz):
            for k in range(1, ny):
                beside(q, h, k).wait_recv()

        totals = piece[q]
        term = lax.dot_general(
            totals, wout_ref[:, cols(q)], (((1,), (1,)), ((), ())),
            preferred_element_type=jnp.float32,
        )

        @pl.when(q == 0)
        def _():
            ctx[...] = term

        @pl.when(q > 0)
        def _():
            ctx[...] += term

        share_of = lax.dot_general(
            context_t[...], totals, (((1,), (0,)), ((), ())),
            preferred_element_type=jnp.float32,
        )

        @pl.when(q < parts - 1)
        def _():
            proj[q] = share_of.astype(jnp.bfloat16)
            to_owner(q).start()

        @pl.when(q == parts - 1)
        def _():
            acc = share_of
            for other in range(parts - 1):
                to_owner(other).wait_recv()
                acc = acc + proj_in[other].astype(jnp.float32)
            proj_ref[...] = acc.astype(jnp.bfloat16)
            ctx_ref[...] = ctx[...].astype(jnp.bfloat16)

    def to_owner(q):
        return remote(
            proj.at[q], proj_in.at[q], proj_s.at[q], proj_r.at[q],
            (owner(q, g), z * ny + y),
        )

    stages = [gathered, total]
    stages += [functools.partial(lambda s, q: forward(q, s), s) for s in range(1, nz)]
    stages += [project]

    last = len(stages) - 1

    def begin(q, carry):
        scatter(q)
        return carry

    lax.fori_loop(0, parts, begin, 0)

    def step(t, carry):
        for k in [*reversed(range(last)), last]:
            @pl.when((t >= k) & (t - k < parts))
            def _():
                stages[k](t - k)

        @pl.when(t == 0)
        def _():
            context_t[...] = context_ref[...].T

        return carry

    lax.fori_loop(0, parts + last, step, 0)

    def drain(q, carry):
        def one(k, c):
            plane(q, k).wait_send()
            return c

        lax.fori_loop(1, planes, one, 0)
        for k in range(1, nz):
            to_height(q, k).wait_send()
        for h in range(nz):
            for k in range(1, ny):
                sideways(q, h, k).wait_send()
        for s in range(nz - 1):
            @pl.when((z - s >= 0) & (z < nz - 1))
            def _():
                up(q, z - s, s).wait_send()

            @pl.when((z + s < nz) & (z > 0))
            def _():
                down(q, z + s, s).wait_send()

        @pl.when(q < parts - 1)
        def _():
            to_owner(q).wait_send()

        return carry

    lax.fori_loop(0, parts, drain, 0)


def collect(row_grad, placer, picker, out_grad, context, w_out, groups, nz, ny):
    rows, width = out_grad.shape
    features = w_out.shape[0]
    taken = placer.shape[0]
    planes = groups * ny
    parts = groups
    chunk = width // parts
    tokens = nz * ny * rows
    dma = pltpu.SemaphoreType.DMA
    vmem = pl.BlockSpec(memory_space=pltpu.VMEM)
    line = (parts, nz * rows, chunk)
    return pl.pallas_call(
        collect_kernel,
        out_shape=(
            jax.ShapeDtypeStruct((tokens, features), jnp.bfloat16),
            jax.ShapeDtypeStruct((features, chunk), jnp.bfloat16),
        ),
        in_specs=[vmem] * 6,
        out_specs=(vmem, vmem),
        scratch_shapes=[
            pltpu.VMEM((parts, taken, chunk), jnp.bfloat16),
            pltpu.VMEM((parts, taken, chunk), jnp.bfloat16),
            pltpu.VMEM(line, jnp.float32),
            pltpu.VMEM((parts, tokens, chunk), jnp.bfloat16),
            pltpu.VMEM((tokens, features), jnp.float32),
            pltpu.VMEM((parts - 1, features, chunk), jnp.bfloat16),
            pltpu.VMEM((parts - 1, features, chunk), jnp.bfloat16),
            pltpu.VMEM(line, jnp.bfloat16),
            pltpu.VMEM(line, jnp.bfloat16),
            pltpu.VMEM((features, tokens), jnp.bfloat16),
            dma((parts, planes - 1)), dma((parts, planes - 1)),
            dma((parts, nz - 1)), dma((parts, nz - 1)),
            dma((parts, nz - 1)), dma((parts, nz - 1)),
            dma((parts, nz - 1)), dma((parts, nz - 1)),
            dma((parts, nz, ny - 1)), dma((parts, nz, ny - 1)),
            dma((parts - 1,)), dma((parts - 1,)),
        ],
        compiler_params=pltpu.CompilerParams(
            collective_id=1, has_side_effects=True, vmem_limit_bytes=44 * 2**20
        ),
    )(row_grad, placer, picker, out_grad, context, w_out)


def expert_backward(rows_in, scaled, gate_pre, up_pre, back_hidden, gate_w, up_w):
    sig = jax.nn.sigmoid(gate_pre)
    silu = gate_pre * sig
    hidden = (silu * up_pre).astype(jnp.bfloat16)
    outer = (((0,), (0,)), ((), ()))
    inner_dims = (((1,), (1,)), ((), ()))
    back_gate = (back_hidden * up_pre * sig * (1.0 + gate_pre * (1.0 - sig))).astype(jnp.bfloat16)
    back_up = (back_hidden * silu).astype(jnp.bfloat16)
    row_grad = lax.dot_general(back_gate, gate_w, inner_dims, preferred_element_type=jnp.float32)
    row_grad = row_grad + lax.dot_general(
        back_up, up_w, inner_dims, preferred_element_type=jnp.float32
    )
    grad_down = lax.dot_general(hidden, scaled, outer, preferred_element_type=jnp.float32).astype(
        jnp.bfloat16
    )
    grad_gate = lax.dot_general(
        rows_in, back_gate, outer, preferred_element_type=jnp.float32
    ).astype(jnp.bfloat16)
    grad_up = lax.dot_general(rows_in, back_up, outer, preferred_element_type=jnp.float32).astype(
        jnp.bfloat16
    )
    return (grad_gate, grad_up, grad_down, row_grad.astype(jnp.bfloat16))


def tables(selected, rows, most):
    groups, nz, ny, g, z, y = place()
    inner = nz * ny
    planes = groups * ny
    cap = selected.shape[1]
    me = g * ny + y
    experts = selected.reshape(groups, nz, ny, cap)
    experts = lax.dynamic_index_in_dim(experts, z, 1, keepdims=False).reshape(planes, cap)
    owner = experts // rows
    owner_z = (owner % inner) // ny
    owner_p = (owner // inner) * ny + owner % ny
    slot_range = jnp.arange(cap, dtype=jnp.int32)
    earlier = (owner[:, :, None] == owner[:, None, :]) & (
        slot_range[None, :, None] > slot_range[None, None, :]
    )
    ranking = jnp.sum(earlier.astype(jnp.int32), axis=2)
    slots = nz * most
    slot = owner_z * most + ranking
    token = owner_z * rows + experts % rows
    hit = (owner_p == me)[:, :, None] & (
        slot[:, :, None] == jnp.arange(slots, dtype=jnp.int32)[None, None, :]
    )
    table = jnp.sum(jnp.where(hit, token[:, :, None] + 1, 0), axis=1).reshape(-1)
    token_ids = jnp.arange(nz * rows, dtype=jnp.int32) + 1
    picker = (table[:, None] == token_ids[None, :]).astype(jnp.bfloat16)
    position = lax.dynamic_index_in_dim(owner_p * slots + slot, me, 0, keepdims=False)
    arrival = jnp.arange(planes * slots, dtype=jnp.int32)
    placer = (position[:, None] == arrival[None, :]).astype(jnp.bfloat16)
    return picker, placer


def body(moe_input, out_grad, context, gate_scale, selected, w_gate, w_up, w_down, w_out):
    groups = lax.axis_size("grp")
    inner_count = lax.axis_size("inner")
    devices = groups * inner_count
    nz, ny = split_inner(inner_count)
    planes = groups * ny
    tok_rows, width = moe_input.shape
    capacity = selected.shape[1]
    most = max(4, (2 * capacity + devices - 1) // devices)
    picker, placer = tables(selected, tok_rows, most)
    rows_in, scaled, gate_pre, up_pre, back_hidden = dispatch(
        moe_input, out_grad, w_gate[0], w_up[0], w_down[0], picker, placer,
        gate_scale[0][:, None], nz, planes,
    )
    grad_gate, grad_up, grad_down, row_grad = expert_backward(
        rows_in, scaled, gate_pre, up_pre, back_hidden, w_gate[0], w_up[0]
    )
    grad_ctx, grad_proj = collect(
        row_grad, placer.T, picker.T, out_grad, context, w_out, groups, nz, ny
    )
    return (
        grad_gate[None],
        grad_up[None],
        grad_down[None],
        grad_ctx,
        grad_proj,
    )


def solution(mesh):
    placed = (
        P(("grp", "inner"), None),
        P(("grp", "inner"), None),
        P("grp", "inner"),
        P(("grp", "inner"), None),
        P(),
        P(("grp", "inner"), None, None),
        P(("grp", "inner"), None, None),
        P(("grp", "inner"), None, None),
        P("inner", None),
    )
    return jax.shard_map(
        body,
        mesh=mesh,
        in_specs=placed,
        out_specs=(
            P(("grp", "inner"), None, None),
            P(("grp", "inner"), None, None),
            P(("grp", "inner"), None, None),
            P("grp", "inner"),
            P("inner", "grp"),
        ),
        check_vma=False,
    )
```
